256 devices in a mesh: chan: 128 (over y, x, z), tm: 2 (over core).
Axes of the slice: x: 4, y: 4, z: 8, core: 2. Of those that a mesh axis runs over, the one named last changes fastest.
Arguments:
- voltages: bfloat16 [2, 384, 1, 256, 2, 1024], P('tm', 'chan'), may hold values from -6 to 6
- filter_taps: float32 [4, 256], replicated, may hold values from -4 to 4
- block_mask: int32 [36, 256], P(None, 'chan'), may hold values 0 or 1
Outputs:
- visibilities: float32 [36, 256, 2, 128, 128], P('tm', 'chan')
The draws below stay inside these ranges and needn't reach their ends.
Inputs may be any that keep to these rules, and one draw needn't show every extreme that they name: `block_mask`: 1 marks a block pair that is correlated in that channel, 0 one that is not.
All inputs are finite; a program needn't handle non-finite values.
Results may differ from the reference program's by a relative error of at most 0.0044.
Values may be sent and summed in bfloat16 or wider, within the bound.
A program may use at most 128 MiB of HBM per device.

```python
import math
import jax
import jax.numpy as jnp
from jax import lax

FINE = 256
COARSE = 1
BLOCK_ST = 64
NBLK = 8
TAPS = 4
FRAMES_DEV = 3
INPUTS = 1024
PAIRS = 36
CHANNELS = 256
FRAMES = 384
N_TM = 2


def place_ends(values, stream_key, low, top_value):
    longest = values.shape.index(max(values.shape))
    spots = []
    for shift in (0, 1):
        where = [jax.random.randint(jax.random.fold_in(stream_key, axis), (), 0, length) for axis, length in enumerate(values.shape)]
        where[longest] = (where[longest] + shift) % values.shape[longest]
        spots.append(tuple(where))
    return values.at[spots[0]].set(low).at[spots[1]].set(top_value)


def shard_levels(stream_key, shape, shards, smallest, largest):
    def one(dim, shards_of):
        heights = jax.random.uniform(jax.random.fold_in(jax.random.fold_in(stream_key, 6), dim), (shards_of,), jnp.float32, smallest / len(shards), largest / len(shards))
        return jnp.repeat(jnp.exp(heights), shape[dim] // shards_of).reshape((-1,) + (1,) * (len(shape) - dim - 1))

    gain = one(*shards[0])
    for cut in shards[1:]:
        gain = gain * one(*cut)
    return gain


def bell_draw(rng, extent, scale, reach, split=(), held_as=jnp.bfloat16):
    values = scale * jax.random.normal(rng, extent, jnp.float32)
    if split:
        values = values * shard_levels(rng, extent, split, -0.22, 0.18)
    return jnp.clip(values, -reach, reach).astype(held_as)


def setup_inputs(seed: int = 0) -> dict:
    splits = jax.random.split(jax.random.key(seed), 4)
    voltages = bell_draw(splits[0], (N_TM, FRAMES, COARSE, FINE, 2, INPUTS), 1.0, 6.0, ((0, 2), (1, 128)))
    filter_taps = bell_draw(splits[1], (TAPS, FINE), (TAPS ** -0.5), 4.0, (), jnp.float32)
    block_mask = place_ends((jax.random.randint(splits[2], (PAIRS, CHANNELS), 0, 3) < 1).astype(jnp.int32), jax.random.fold_in(splits[2], 1), 0, 1)
    return {"voltages": voltages, "filter_taps": filter_taps, "block_mask": block_mask}


def dft_table(size):
    index = jnp.arange(size, dtype=jnp.int32)
    product = index[:, None] * index[None, :] % size
    angle = product.astype(jnp.float32) * (2.0 * math.pi / size)
    cosine = jnp.cos(angle) / math.sqrt(size)
    sine = jnp.sin(angle) / math.sqrt(size)
    upper = jnp.stack([cosine, sine], 2)
    lower = jnp.stack([-sine, cosine], 2)
    return jnp.stack([upper, lower], 1).reshape(2 * size, 2 * size).astype(jnp.bfloat16)

def spectra_of(extended, filter_taps, table):
    count = extended.shape[0] - (TAPS - 1)
    weighted = jnp.zeros((count,) + extended.shape[1:], jnp.float32)
    for p in range(TAPS):
        piece = extended[TAPS - 1 - p:TAPS - 1 - p + count].astype(jnp.float32)
        weighted = weighted + filter_taps[p][None, None, :, None, None] * piece
    weighted = weighted.astype(jnp.bfloat16)
    shape = weighted.shape
    flat = weighted.reshape(shape[0], shape[1], 2 * shape[2], shape[4])
    result = jnp.einsum('kn,fgni->fgki', table.astype(jnp.float32), flat.astype(jnp.float32))
    return result.astype(jnp.bfloat16).reshape(shape[0], shape[1] * shape[2], 2, shape[4])

def channel_pairs(series):
    width = 2 * BLOCK_ST
    values = series.astype(jnp.float32)
    blocks = []
    for first in range(NBLK):
        left = values[:, :, first * width:(first + 1) * width]
        right = values[:, :, first * width:]
        rotated = jnp.stack([jnp.stack([right[:, 0], -right[:, 1]], 1), jnp.stack([right[:, 1], right[:, 0]], 1)], 1)
        product = jnp.einsum('fci,fcsj->sij', left, rotated)
        for second in range(NBLK - first):
            blocks.append(product[:, :, second * width:(second + 1) * width])
    return jnp.stack(blocks, 0)

def reference(voltages, filter_taps, block_mask):
    table = dft_table(FINE)
    subs = []
    for sub in range(voltages.shape[0]):
        frames = voltages[sub]
        history = jnp.zeros((TAPS - 1,) + frames.shape[1:], jnp.bfloat16)
        padded = jnp.concatenate([history, frames], 0)
        step_len = FRAMES_DEV

        def one_block(begin):
            piece = lax.dynamic_slice_in_dim(padded, begin, step_len + TAPS - 1, 0)
            return spectra_of(piece, filter_taps, table)
        starts = (jnp.arange(frames.shape[0] // step_len) * step_len).astype(jnp.int32)
        stacked = lax.map(one_block, starts)
        subs.append(stacked.reshape((frames.shape[0],) + stacked.shape[2:]))
    everything = jnp.concatenate(subs, 0)
    by_channel = jnp.transpose(everything, (1, 0, 2, 3))
    sums = lax.map(channel_pairs, by_channel)
    sums = jnp.transpose(sums, (1, 0, 2, 3, 4))
    scale = 1.0 / math.sqrt(everything.shape[0])
    weights = block_mask.astype(jnp.float32)[:, :, None, None, None]
    return sums * weights * scale
```

```python
import functools
import math

import jax
import jax.numpy as jnp
import numpy as np
from jax import lax
from jax.experimental import pallas as pl
from jax.experimental.pallas import tpu as pltpu
from jax.sharding import PartitionSpec as P

TAPS = 4
FRAMES = 3
TILE = 128
NBLK = 8
STEPS = 4
MESH = pl.DeviceIdType.MESH
BF16 = jnp.bfloat16
F32 = jnp.float32

PAIRS = [(a, b) for a in range(NBLK) for b in range(a, NBLK)]


def dft_table(size):
    index = np.arange(size)
    angle = (index[:, None] * index[None, :] % size).astype(np.float32) * np.float32(2.0 * math.pi / size)
    cosine = np.cos(angle) / np.float32(math.sqrt(size))
    sine = np.sin(angle) / np.float32(math.sqrt(size))
    upper = np.stack([cosine, sine], 2)
    lower = np.stack([-sine, cosine], 2)
    table = np.stack([upper, lower], 1).reshape(size // 2, 2, 2, 2 * size)
    table = np.transpose(table, (1, 0, 2, 3)).reshape(2, size, 2 * size)
    return jnp.asarray(table.astype(BF16))


def turn_table(size):
    turn = np.zeros((size, size), np.float32)
    even = np.arange(0, size, 2)
    turn[even + 1, even] = 1.0
    turn[even, even + 1] = -1.0
    return jnp.asarray(turn.astype(BF16))


def pairs_ready(step, half):
    fresh = (step, step + STEPS)
    ready = []
    for a, b in PAIRS[half * 18 : half * 18 + 18]:
        if a % STEPS <= step and b % STEPS <= step and (a in fresh or b in fresh):
            ready.append((a, b))
    return ready


def digits(values):
    total = 0
    for place, value in enumerate(values):
        total += value * 8**place
    return total


def merged(ref):
    shape = ref.shape
    return ref.reshape(shape[:-3] + (shape[-3] * shape[-2], shape[-1]))


def kernel(
    count,
    v_ref, taps_ref, table_ref, turn_ref, weight_ref, out_ref,
    own, before, after, weighted, send, recv, other, left,
    load_sem, near_send, near_recv, send_sem, recv_sem, core_send, core_recv,
):
    me = lax.axis_index("chan")
    core = lax.axis_index("tm")
    fine = 2 * count
    rows = 2 * fine
    depth = 2 * FRAMES * count
    half = lax.rem(me, 2)
    up = lax.rem(me + 1, count)
    down = lax.rem(me + count - 1, count)

    own_rows, before_rows, after_rows = merged(own), merged(before), merged(after)
    send_rows, recv_rows, other_rows = merged(send), merged(recv), merged(other)

    def load(block):
        lanes = pl.ds(pl.multiple_of(block * TILE, TILE), TILE)
        return pltpu.make_async_copy(v_ref.at[:, :, :, lanes], own.at[block], load_sem.at[block])

    for step in range(STEPS):
        load((1 - half) * STEPS + step).start()
    for step in range(STEPS):
        load(half * STEPS + step).start()

    barrier = pltpu.get_barrier_semaphore()

    def greet(offset, carry):
        peer = lax.rem(me + offset, count)
        pl.semaphore_signal(barrier, inc=1, device_id={"chan": peer}, device_id_type=MESH)
        return carry

    lax.fori_loop(1, count, greet, 0)
    pl.semaphore_signal(barrier, inc=1, device_id={"tm": 1 - core}, device_id_type=MESH)
    pl.semaphore_wait(barrier, count)

    def near(step):
        block = (1 - half) * STEPS + step
        forward = pltpu.make_async_remote_copy(
            own.at[block], before.at[step], near_send.at[step, 0], near_recv.at[step, 0],
            device_id={"chan": up}, device_id_type=MESH,
        )
        backward = pltpu.make_async_remote_copy(
            own.at[block], after.at[step], near_send.at[step, 1], near_recv.at[step, 1],
            device_id={"chan": down}, device_id_type=MESH,
        )
        return forward, backward

    for step in range(STEPS):
        load((1 - half) * STEPS + step).wait()
        forward, backward = near(step)
        forward.start()
        backward.start()

    keep_before = jnp.where(me == 0, 0.0, 1.0).astype(F32)
    keep_own = jnp.where(me == count - 1, 0.0, 1.0).astype(F32)
    group = 16

    def across(step):
        return pltpu.make_async_remote_copy(
            recv.at[step], other.at[step], core_send.at[step], core_recv.at[step],
            device_id={"tm": 1 - core}, device_id_type=MESH,
        )

    for step in range(STEPS):
        block = half * STEPS + step
        load(block).wait()
        for copy in near(step):
            copy.wait_recv()

        def filter_rows(index, carry):
            at = pl.ds(pl.multiple_of(index * group, group), group)
            series = [before_rows[step, f, at, :].astype(F32) for f in range(FRAMES)]
            series += [own_rows[block, f, at, :].astype(F32) for f in range(FRAMES)]
            series += [after_rows[step, f, at, :].astype(F32) for f in range(FRAMES)]
            taps = [taps_ref[p, at, :] for p in range(TAPS)]
            for f in range(2 * FRAMES):
                inside = f % FRAMES
                total = taps[0] * series[FRAMES + f]
                for p in range(1, inside + 1):
                    total = total + taps[p] * series[FRAMES + f - p]
                past = taps[inside + 1] * series[FRAMES + f - inside - 1]
                for p in range(inside + 2, TAPS):
                    past = past + taps[p] * series[FRAMES + f - p]
                total = total + past * (keep_before if f < FRAMES else keep_own)
                weighted[at, f * TILE : (f + 1) * TILE] = total.astype(BF16)
            return carry

        lax.fori_loop(0, rows // group, filter_rows, 0)

        for parity in range(2):
            for pair in range(FRAMES):
                part = jnp.dot(
                    table_ref[parity], weighted[:, pair * 2 * TILE : (pair + 1) * 2 * TILE],
                    preferred_element_type=F32,
                ).astype(BF16)
                send_rows[step, parity, 2 * pair] = part[:, :TILE]
                send_rows[step, parity, 2 * pair + 1] = part[:, TILE:]

        @pl.when(me < count - 1)
        def _():
            place = pl.ds(3 * me, 2 * FRAMES)
            pltpu.make_async_copy(
                send.at[step, :, :, me], recv.at[step, half, :, place], recv_sem.at[step]
            ).start()

            def turn(offset, carry):
                peer = lax.rem(me + offset, count)
                pltpu.make_async_remote_copy(
                    send.at[step, :, :, peer], recv.at[step, half, :, place],
                    send_sem.at[step], recv_sem.at[step],
                    device_id={"chan": peer}, device_id_type=MESH,
                ).start()
                return carry

            lax.fori_loop(1, count, turn, 0)

        @pl.when(me == count - 1)
        def _():
            for first, place in ((0, FRAMES * count - FRAMES), (FRAMES, 0)):
                source = pl.ds(first, FRAMES)
                target = pl.ds(place, FRAMES)
                pltpu.make_async_copy(
                    send.at[step, :, source, count - 1], recv.at[step, 1, :, target], recv_sem.at[step]
                ).start()

                def turn(peer, carry):
                    pltpu.make_async_remote_copy(
                        send.at[step, :, source, peer], recv.at[step, 1, :, target],
                        send_sem.at[step], recv_sem.at[step],
                        device_id={"chan": peer}, device_id_type=MESH,
                    ).start()
                    return carry

                lax.fori_loop(0, count - 1, turn, 0)

    span = min(256, depth)

    def turn_block(step, side, source, base):
        block = side * STEPS + step

        def one(index, carry):
            parity = index // (depth // span)
            piece = lax.rem(index, depth // span)
            at = pl.ds(pl.multiple_of(piece * span, span), span)
            to = pl.ds(pl.multiple_of(base + piece * span, span), span)
            flat = source[step, side, parity, at, :].T
            left[block, parity, 0:TILE, to] = flat
            left[block, parity, TILE : 2 * TILE, to] = jnp.dot(
                flat, turn_ref[...], preferred_element_type=F32
            ).astype(BF16)
            return carry

        lax.fori_loop(0, 2 * (depth // span), one, 0)

    def turn_blocks(step, source, base):
        for side in range(2):
            block = side * STEPS + step
            if block == 2:
                turn_block(step, side, source, base)
            else:
                @pl.when(core == (0 if block < 2 else 1))
                def _():
                    turn_block(step, side, source, base)

    for step in range(STEPS):
        pltpu.make_async_copy(recv.at[step], recv.at[step], recv_sem.at[step]).wait()
        across(step).start()
        turn_blocks(step, recv_rows, 0)
        across(step).wait_recv()
        turn_blocks(step, other_rows, depth)

        lists = [pairs_ready(step, 0), pairs_ready(step, 1)]
        firsts = [digits([a for a, _ in pairs]) for pairs in lists]
        seconds = [digits([b for _, b in pairs]) for pairs in lists]

        def one_pair(index, carry):
            first_code, second_code = carry
            a = lax.rem(first_code, 8)
            b = lax.rem(second_code, 8)
            slot = a * NBLK - a * (a - 1) // 2 + b - a
            b_step = lax.rem(b, STEPS)
            b_side = b // STEPS
            for parity in range(2):
                sums = jnp.dot(
                    left[a, parity, :, 0:depth], recv_rows[b_step, b_side, parity],
                    preferred_element_type=F32,
                ) + jnp.dot(
                    left[a, parity, :, depth : 2 * depth], other_rows[b_step, b_side, parity],
                    preferred_element_type=F32,
                )
                sums = sums * weight_ref[slot, parity]
                out_ref[slot - 18 * core, parity, 0] = sums[:TILE]
                out_ref[slot - 18 * core, parity, 1] = sums[TILE:]
            return first_code // 8, second_code // 8

        total = len(lists[0]) + core * (len(lists[1]) - len(lists[0]))
        lax.fori_loop(
            0, total, one_pair,
            (firsts[0] + core * (firsts[1] - firsts[0]), seconds[0] + core * (seconds[1] - seconds[0])),
        )

    for step in range(STEPS):
        sent = send.at[step, :, :, pl.ds(0, count - 1)]
        pltpu.make_async_copy(sent, sent, send_sem.at[step]).wait()
        for copy in near(step):
            copy.wait_send()
        across(step).wait_send()


def per_device(count, voltages, filter_taps, block_mask):
    fine = 2 * count
    frames = voltages.reshape(FRAMES, fine, 2, NBLK * TILE)
    taps = jnp.broadcast_to(jnp.repeat(filter_taps, 2, 1)[:, :, None], (TAPS, 2 * fine, TILE))
    weights = block_mask.astype(F32) * F32(1.0 / math.sqrt(FRAMES * count * 2))
    depth = 2 * FRAMES * count
    dma = pltpu.SemaphoreType.DMA
    vmem = pl.BlockSpec(memory_space=pltpu.VMEM)
    return pl.pallas_call(
        functools.partial(kernel, count),
        out_shape=jax.ShapeDtypeStruct((18, 2, 2, TILE, TILE), F32),
        in_specs=[
            pl.BlockSpec(memory_space=pl.ANY), vmem, vmem, vmem,
            pl.BlockSpec(memory_space=pltpu.SMEM),
        ],
        out_specs=vmem,
        scratch_shapes=[
            pltpu.VMEM((NBLK, FRAMES, fine, 2, TILE), BF16),
            pltpu.VMEM((STEPS, FRAMES, fine, 2, TILE), BF16),
            pltpu.VMEM((STEPS, FRAMES, fine, 2, TILE), BF16),
            pltpu.VMEM((2 * fine, 2 * FRAMES * TILE), BF16),
            pltpu.VMEM((STEPS, 2, 2 * FRAMES, count, 2, TILE), BF16),
            pltpu.VMEM((STEPS, 2, 2, FRAMES * count, 2, TILE), BF16),
            pltpu.VMEM((STEPS, 2, 2, FRAMES * count, 2, TILE), BF16),
            pltpu.VMEM((NBLK, 2, 2 * TILE, 2 * depth), BF16),
            dma((NBLK,)), dma((STEPS, 2)), dma((STEPS, 2)), dma((STEPS,)), dma((STEPS,)),
            dma((STEPS,)), dma((STEPS,)),
        ],
        compiler_params=pltpu.CompilerParams(
            collective_id=0, has_side_effects=True, vmem_limit_bytes=50 * 2**20
        ),
        cost_estimate=pl.CostEstimate(flops=6 * 10**9, bytes_accessed=10**7, transcendentals=0),
        name="correlate",
    )(frames, taps, dft_table(fine), turn_table(min(256, depth)), weights)


def solution(mesh):
    in_specs = (P("tm", "chan", None, None, None, None), P(), P(None, "chan"))
    out_specs = P("tm", "chan", None, None, None)
    return jax.shard_map(
        functools.partial(per_device, mesh.shape["chan"]),
        mesh=mesh, in_specs=in_specs, out_specs=out_specs, check_vma=False,
    )
```

```python
import functools
import math

import jax
import jax.numpy as jnp
import numpy as np
from jax import lax
from jax.experimental import pallas as pl
from jax.experimental.pallas import tpu as pltpu
from jax.sharding import PartitionSpec as P

TAPS = 4
FRAMES = 3
TILE = 128
NBLK = 8
STEPS = 4
MESH = pl.DeviceIdType.MESH
BF16 = jnp.bfloat16
F32 = jnp.float32

PAIRS = [(a, b) for a in range(NBLK) for b in range(a, NBLK)]


def in_tiles(table):
    width = min(TILE, table.shape[-1])
    table = table.reshape(table.shape[:-2] + (table.shape[-2] // 2, 2, table.shape[-1] // width, width))
    return jnp.asarray(np.moveaxis(table, -2, -4).astype(BF16))


def whole(ref, *index):
    flat = merged(ref)
    return jnp.concatenate([flat[index + (tile,)] for tile in range(flat.shape[len(index)])], 1)


def dft_table(size):
    index = np.arange(size)
    angle = (index[:, None] * index[None, :] % size).astype(np.float32) * np.float32(2.0 * math.pi / size)
    cosine = np.cos(angle) / np.float32(math.sqrt(size))
    sine = np.sin(angle) / np.float32(math.sqrt(size))
    upper = np.stack([cosine, sine], 2)
    lower = np.stack([-sine, cosine], 2)
    table = np.stack([upper, lower], 1).reshape(size // 2, 2, 2, 2 * size)
    table = np.transpose(table, (1, 0, 2, 3)).reshape(2, size, 2 * size)
    return in_tiles(table)


def turn_table(size):
    turn = np.zeros((size, size), np.float32)
    even = np.arange(0, size, 2)
    turn[even + 1, even] = 1.0
    turn[even, even + 1] = -1.0
    return in_tiles(turn)


BLOCKS = ((0, 1, 3, 2), (5, 6, 7, 4))
PARTS = ((0, 1, 0, 2), (1, 2, 0, 2), (3, 1, 0, 1), (3, 1, 1, 1))


def place_of(block):
    half = block // STEPS
    return half * STEPS + BLOCKS[half].index(block)


def units_of(part, core):
    first, positions = PARTS[part][:2]
    ready = range(first + positions)
    fresh = range(first, first + positions)
    units = []
    for a in range(NBLK):
        row = []
        for b in range(a, NBLK):
            slot = PAIRS.index((a, b)) - 18 * core
            at = (place_of(a) % STEPS, place_of(b) % STEPS)
            if 0 <= slot < 18 and max(at) in fresh and max(at) in ready:
                row.append((b, slot))
        if len(row) % 2:
            row.append(row[-1])
        for (b, slot), (c, other) in zip(row[::2], row[1::2]):
            units.append((place_of(a), place_of(b), place_of(c), slot, other))
    return units


def codes_of(part):
    units = [units_of(part, core) for core in range(2)]
    count = max(len(units[0]), len(units[1]))
    codes = []
    for mine in units:
        while len(mine) < count:
            index = next(i for i, unit in enumerate(mine) if unit[3] != unit[4])
            a, b, c, slot, other = mine[index]
            mine[index : index + 1] = [(a, b, b, slot, slot), (a, c, c, other, other)]
        codes.append([
            sum(unit[field] * base**place for place, unit in enumerate(mine))
            for field, base in enumerate((8, 8, 8, 32, 32))
        ])
    return count, codes


def merged(ref):
    shape = ref.shape
    return ref.reshape(shape[:-3] + (shape[-3] * shape[-2], shape[-1]))


def kernel(
    count,
    v_ref, taps_ref, table_hbm, turn_hbm, mask_ref, out_ref,
    own, before, after, taps_wide, table_ref, turn_ref, weighted, send, recv, other, left,
    load_sem, const_sem, near_send, near_recv, send_sem, recv_sem, core_send, core_recv,
):
    me = lax.axis_index("chan")
    core = lax.axis_index("tm")
    fine = 2 * count
    rows = 2 * fine
    depth = 2 * FRAMES * count
    half = lax.rem(me, 2)
    up = lax.rem(me + 1, count)
    down = lax.rem(me + count - 1, count)
    scale = 1.0 / math.sqrt(FRAMES * count * 2)

    own_rows, before_rows, after_rows = merged(own), merged(before), merged(after)
    send_rows, recv_rows, other_rows = merged(send), merged(recv), merged(other)

    def place(away, position):
        side = 1 - half if away else half
        return side * STEPS + position

    def load(away, position):
        index = place(away, position)
        side = 1 - half if away else half
        block = BLOCKS[0][position] + side * (BLOCKS[1][position] - BLOCKS[0][position])
        lanes = pl.ds(pl.multiple_of(block * TILE, TILE), TILE)
        return pltpu.make_async_copy(v_ref.at[:, :, :, lanes], own.at[index], load_sem.at[index])

    constants = (
        pltpu.make_async_copy(table_hbm, table_ref, const_sem.at[0]),
        pltpu.make_async_copy(turn_hbm, turn_ref, const_sem.at[1]),
    )
    for away in (True, False):
        for position in range(STEPS):
            load(away, position).start()
    for copy in constants:
        copy.start()

    barrier = pltpu.get_barrier_semaphore()

    def greet(offset, carry):
        peer = lax.rem(me + offset, count)
        pl.semaphore_signal(barrier, inc=1, device_id={"chan": peer}, device_id_type=MESH)
        return carry

    lax.fori_loop(1, count, greet, 0)
    pl.semaphore_signal(barrier, inc=1, device_id={"tm": 1 - core}, device_id_type=MESH)

    row = lax.broadcasted_iota(jnp.int32, (rows, fine), 0)
    column = lax.broadcasted_iota(jnp.int32, (rows, fine), 1)
    spread = (row // 2 == column).astype(F32)
    for p in range(TAPS):
        wide = jnp.broadcast_to(taps_ref[p : p + 1, :], (TILE, fine))
        taps_wide[p] = lax.dot_general(
            spread, wide, (((1,), (1,)), ((), ())),
            precision=lax.Precision.HIGHEST, preferred_element_type=F32,
        )

    pl.semaphore_wait(barrier, count)

    def near(position):
        source = own.at[place(True, position)]
        return [
            pltpu.make_async_remote_copy(
                source, target.at[position], near_send.at[position, way], near_recv.at[position, way],
                device_id={"chan": peer}, device_id_type=MESH,
            )
            for way, (target, peer) in enumerate(((before, up), (after, down)))
        ]

    for position in range(STEPS):
        load(True, position).wait()
        for copy in near(position):
            copy.start()

    keep_before = jnp.where(me == 0, 0.0, 1.0).astype(F32)
    keep_own = jnp.where(me == count - 1, 0.0, 1.0).astype(F32)
    group = 16

    def filter_position(position):
        index = place(False, position)

        def filter_rows(step, carry):
            at = pl.ds(pl.multiple_of(step * group, group), group)
            series = [before_rows[position, f, at, :].astype(F32) for f in range(FRAMES)]
            series += [own_rows[index, f, at, :].astype(F32) for f in range(FRAMES)]
            series += [after_rows[position, f, at, :].astype(F32) for f in range(FRAMES)]
            taps = [taps_wide[p, at, :] for p in range(TAPS)]
            for f in range(2 * FRAMES):
                inside = f % FRAMES
                total = taps[0] * series[FRAMES + f]
                for p in range(1, inside + 1):
                    total = total + taps[p] * series[FRAMES + f - p]
                past = taps[inside + 1] * series[FRAMES + f - inside - 1]
                for p in range(inside + 2, TAPS):
                    past = past + taps[p] * series[FRAMES + f - p]
                total = total + past * (keep_before if f < FRAMES else keep_own)
                weighted[at, f * TILE : (f + 1) * TILE] = total.astype(BF16)
            return carry

        lax.fori_loop(0, rows // group, filter_rows, 0)

    def transform(position, parity):
        table = whole(table_ref, parity)
        for pair in range(FRAMES):
            part = jnp.dot(
                table, weighted[:, pair * 2 * TILE : (pair + 1) * 2 * TILE],
                preferred_element_type=F32,
            ).astype(BF16)
            send_rows[position, parity, 2 * pair] = part[:, :TILE]
            send_rows[position, parity, 2 * pair + 1] = part[:, TILE:]

    def extent(part):
        first, positions, channel, channels = PARTS[part]
        return pl.ds(first, positions), pl.ds(channel, channels)

    def send_part(part):
        at, channels = extent(part)

        def deliver(source_frames, side, frames):
            target = recv.at[at, side, channels, frames]
            pltpu.make_async_copy(
                send.at[at, channels, source_frames, me], target, recv_sem.at[part]
            ).start()

            def turn(offset, carry):
                peer = lax.rem(me + offset, count)
                pltpu.make_async_remote_copy(
                    send.at[at, channels, source_frames, peer], target,
                    send_sem.at[part], recv_sem.at[part],
                    device_id={"chan": peer}, device_id_type=MESH,
                ).start()
                return carry

            lax.fori_loop(1, count, turn, 0)

        @pl.when(me < count - 1)
        def _():
            deliver(pl.ds(0, 2 * FRAMES), half, pl.ds(FRAMES * me, 2 * FRAMES))

        @pl.when(me == count - 1)
        def _():
            deliver(pl.ds(0, FRAMES), 1, pl.ds(FRAMES * (count - 1), FRAMES))
            deliver(pl.ds(FRAMES, FRAMES), 1, pl.ds(0, FRAMES))

    for position in range(STEPS):
        load(False, position).wait()
        for copy in near(position):
            copy.wait_recv()
        filter_position(position)
        if position == 0:
            constants[0].wait()
        for parity in range(2):
            transform(position, parity)
            for part, (first, positions, channel, channels) in enumerate(PARTS):
                if first + positions - 1 == position and channel + channels - 1 == parity:
                    send_part(part)
    constants[1].wait()

    span = min(256, depth)

    def across(part):
        at, channels = extent(part)
        return pltpu.make_async_remote_copy(
            recv.at[at, :, channels], other.at[at, :, channels], core_send.at[part], core_recv.at[part],
            device_id={"tm": 1 - core}, device_id_type=MESH,
        )

    def turn_part(part, source, base):
        first, positions, channel, channels = PARTS[part]

        def turn_block(position, side):
            def one(parity, carry):
                for piece in range(depth // span):
                    flat = source[position, side, parity, piece * span : (piece + 1) * span, :].T
                    to = slice(base + piece * span, base + (piece + 1) * span)
                    left[side * STEPS + position, parity, 0:TILE, to] = flat
                    left[side * STEPS + position, parity, TILE : 2 * TILE, to] = jnp.dot(
                        flat, whole(turn_ref), preferred_element_type=F32
                    ).astype(BF16)
                return carry

            lax.fori_loop(channel, channel + channels, one, 0)

        for position in range(first, first + positions):
            for side in range(2):
                block = BLOCKS[side][position]
                if block == 2:
                    turn_block(position, side)
                else:
                    pl.when(core == (0 if block < 2 else 1))(functools.partial(turn_block, position, side))

    def multiply_part(part, source, base):
        first, positions, channel, channels = PARTS[part]
        total, codes = codes_of(part)

        def one_unit(step, carry):
            a, b, c = (lax.rem(code, 8) for code in carry[:3])
            slots = [lax.rem(code, 32) for code in carry[3:]]
            for parity in range(channel, channel + channels):
                right = jnp.concatenate(
                    [source[lax.rem(at, STEPS), at // STEPS, parity] for at in (b, c)], 1
                )
                sums = jnp.dot(left[a, parity, :, base : base + depth], right, preferred_element_type=F32)
                parts = []
                for index, slot in enumerate(slots):
                    weight = mask_ref[parity, slot + 18 * core].astype(F32) * scale
                    one = sums[:, index * TILE : (index + 1) * TILE].reshape(2, TILE, TILE) * weight
                    parts.append(one + out_ref[slot, parity] if base else one)
                for slot, one in zip(slots, parts):
                    out_ref[slot, parity] = one
            return tuple(code // 8 for code in carry[:3]) + tuple(code // 32 for code in carry[3:])

        start = tuple(low + core * (high - low) for low, high in zip(*codes))
        lax.fori_loop(0, total, one_unit, start, unroll=total if channels == 1 else 1)

    for part in range(len(PARTS)):
        at, channels = extent(part)
        arrived = recv.at[at, :, channels]
        pltpu.make_async_copy(arrived, arrived, recv_sem.at[part]).wait()
        across(part).start()
        turn_part(part, recv_rows, 0)
        multiply_part(part, recv_rows, 0)
        across(part).wait_recv()
        turn_part(part, other_rows, depth)
        multiply_part(part, other_rows, depth)

    for part in range(len(PARTS)):
        at, channels = extent(part)
        sent = send.at[at, channels, :, pl.ds(0, count - 1)]
        pltpu.make_async_copy(sent, sent, send_sem.at[part]).wait()
        across(part).wait_send()
    for position in range(STEPS):
        for copy in near(position):
            copy.wait_send()


def per_device(count, voltages, filter_taps, block_mask):
    fine = 2 * count
    frames = voltages.reshape(FRAMES, fine, 2, NBLK * TILE)
    depth = 2 * FRAMES * count
    span = min(256, depth)
    table, rotation = dft_table(fine), turn_table(span)
    dma = pltpu.SemaphoreType.DMA
    vmem = pl.BlockSpec(memory_space=pltpu.VMEM)
    anywhere = pl.BlockSpec(memory_space=pl.ANY)
    parts = len(PARTS)
    return pl.pallas_call(
        functools.partial(kernel, count),
        out_shape=pltpu.VMEM((18, 2, 2, TILE, TILE), F32),
        in_specs=[anywhere, vmem, anywhere, anywhere, pl.BlockSpec(memory_space=pltpu.SMEM)],
        out_specs=vmem,
        scratch_shapes=[
            pltpu.VMEM((NBLK, FRAMES, fine, 2, TILE), BF16),
            pltpu.VMEM((STEPS, FRAMES, fine, 2, TILE), BF16),
            pltpu.VMEM((STEPS, FRAMES, fine, 2, TILE), BF16),
            pltpu.VMEM((TAPS, 2 * fine, TILE), F32),
            pltpu.VMEM(table.shape, BF16),
            pltpu.VMEM(rotation.shape, BF16),
            pltpu.VMEM((2 * fine, 2 * FRAMES * TILE), BF16),
            pltpu.VMEM((STEPS, 2, 2 * FRAMES, count, 2, TILE), BF16),
            pltpu.VMEM((STEPS, 2, 2, FRAMES * count, 2, TILE), BF16),
            pltpu.VMEM((STEPS, 2, 2, FRAMES * count, 2, TILE), BF16),
            pltpu.VMEM((NBLK, 2, 2 * TILE, 2 * depth), BF16),
            dma((NBLK,)), dma((2,)), dma((STEPS, 2)), dma((STEPS, 2)), dma((parts,)), dma((parts,)),
            dma((parts,)), dma((parts,)),
        ],
        compiler_params=pltpu.CompilerParams(
            collective_id=0, has_side_effects=True, vmem_limit_bytes=50 * 2**20
        ),
        cost_estimate=pl.CostEstimate(flops=6 * 10**9, bytes_accessed=10**7, transcendentals=0),
        name="correlate",
    )(frames, filter_taps, table, rotation, block_mask.T)


def solution(mesh):
    in_specs = (P("tm", "chan", None, None, None, None), P(), P(None, "chan"))
    out_specs = P("tm", "chan", None, None, None)
    return jax.shard_map(
        functools.partial(per_device, mesh.shape["chan"]),
        mesh=mesh, in_specs=in_specs, out_specs=out_specs, check_vma=False,
    )
```

```python
import functools
import math

import jax
import jax.numpy as jnp
import numpy as np
from jax import lax
from jax.experimental import pallas as pl
from jax.experimental.pallas import tpu as pltpu
from jax.sharding import PartitionSpec as P

TAPS = 4
FRAMES = 3
TILE = 128
NBLK = 8
STEPS = 4
RING = 8
REACH = 4
MESH = pl.DeviceIdType.MESH
BF16 = jnp.bfloat16
F32 = jnp.float32

PAIRS = [(a, b) for a in range(NBLK) for b in range(a, NBLK)]


def in_tiles(table):
    width = min(TILE, table.shape[-1])
    table = table.reshape(table.shape[:-2] + (table.shape[-2] // 2, 2, table.shape[-1] // width, width))
    return jnp.asarray(np.moveaxis(table, -2, -4).astype(BF16))


def whole(ref, *index):
    flat = merged(ref)
    return jnp.concatenate([flat[index + (tile,)] for tile in range(flat.shape[len(index)])], 1)


def dft_table(size):
    index = np.arange(size)
    angle = (index[:, None] * index[None, :] % size).astype(np.float32) * np.float32(2.0 * math.pi / size)
    cosine = np.cos(angle) / np.float32(math.sqrt(size))
    sine = np.sin(angle) / np.float32(math.sqrt(size))
    upper = np.stack([cosine, sine], 2)
    lower = np.stack([-sine, cosine], 2)
    plane = size // 2 // RING
    table = np.stack([upper, lower], 1).reshape(plane, RING, 2, 2, 2 * size)
    table = np.transpose(table, (1, 2, 0, 3, 4)).reshape(RING, 2, 2 * plane, 2 * size)
    return in_tiles(table)


def turn_table(size):
    turn = np.zeros((size, size), np.float32)
    even = np.arange(0, size, 2)
    turn[even + 1, even] = 1.0
    turn[even, even + 1] = -1.0
    return in_tiles(turn)


BLOCKS = ((0, 1, 3, 2), (5, 6, 7, 4))
PARTS = ((0, 1, 0, 2), (1, 2, 0, 2), (3, 1, 0, 1), (3, 1, 1, 1))


def place_of(block):
    half = block // STEPS
    return half * STEPS + BLOCKS[half].index(block)


def units_of(part, core):
    first, positions = PARTS[part][:2]
    ready = range(first + positions)
    fresh = range(first, first + positions)
    units = []
    for a in range(NBLK):
        row = []
        for b in range(a, NBLK):
            slot = PAIRS.index((a, b)) - 18 * core
            at = (place_of(a) % STEPS, place_of(b) % STEPS)
            if 0 <= slot < 18 and max(at) in fresh and max(at) in ready:
                row.append((b, slot))
        if len(row) % 2:
            row.append(row[-1])
        for (b, slot), (c, other) in zip(row[::2], row[1::2]):
            units.append((place_of(a), place_of(b), place_of(c), slot, other))
    return units


def codes_of(part):
    units = [units_of(part, core) for core in range(2)]
    count = max(len(units[0]), len(units[1]))
    codes = []
    for mine in units:
        while len(mine) < count:
            index = next(i for i, unit in enumerate(mine) if unit[3] != unit[4])
            a, b, c, slot, other = mine[index]
            mine[index : index + 1] = [(a, b, b, slot, slot), (a, c, c, other, other)]
        codes.append([
            sum(unit[field] * base**place for place, unit in enumerate(mine))
            for field, base in enumerate((8, 8, 8, 32, 32))
        ])
    return count, codes


def merged(ref):
    shape = ref.shape
    return ref.reshape(shape[:-3] + (shape[-3] * shape[-2], shape[-1]))


def kernel(
    count,
    v_ref, taps_ref, table_hbm, turn_hbm, mask_ref, out_ref,
    own, taps_wide, table_ref, turn_ref, weighted, part_send, part_recv, send, recv, other, left,
    load_sem, const_sem, near_send, near_recv, send_sem, recv_sem, core_send, core_recv,
):
    me = lax.axis_index("chan")
    core = lax.axis_index("tm")
    fine = 2 * count
    rows = 2 * fine
    depth = 2 * FRAMES * count
    plane = count // RING
    near_rows = 2 * REACH * plane
    here = lax.rem(me, RING)
    column = me // RING
    up = lax.rem(me + 1, count)
    down = lax.rem(me + count - 1, count)
    scale = 1.0 / math.sqrt(FRAMES * count * 2)

    own_rows, table_rows = merged(own), merged(table_ref)
    part_send_rows, part_recv_rows = merged(part_send), merged(part_recv)
    send_rows, recv_rows, other_rows = merged(send), merged(recv), merged(other)

    def load(position, side):
        block = BLOCKS[side][position]
        index = side * STEPS + position
        lanes = pl.ds(block * TILE, TILE)
        return pltpu.make_async_copy(v_ref.at[:, :, :, lanes], own.at[index], load_sem.at[index])

    for position in range(STEPS):
        for side in range(2):
            load(position, side).start()
    for entry in range(RING + 1):
        pltpu.make_async_copy(
            table_hbm.at[lax.rem(here + entry + RING - REACH, RING)],
            table_ref.at[:, :, pl.ds(entry * plane, plane)], const_sem.at[0],
        ).start()
    turn_copy = pltpu.make_async_copy(turn_hbm, turn_ref, const_sem.at[1])
    turn_copy.start()

    def chip(along, across):
        return lax.rem(column + across, plane) * RING + lax.rem(here + along + RING, RING)

    barrier = pltpu.get_barrier_semaphore()

    def greet(index, carry):
        along = index // plane
        peer = chip(along + along // REACH, lax.rem(index, plane))
        pl.semaphore_signal(barrier, inc=1, device_id={"chan": peer}, device_id_type=MESH)
        return carry

    greeted = (RING - 1) * plane
    lax.fori_loop(1, greeted, greet, 0)
    pl.semaphore_signal(barrier, inc=1, device_id={"tm": 1 - core}, device_id_type=MESH)

    row = lax.broadcasted_iota(jnp.int32, (rows, fine), 0)
    sample = lax.broadcasted_iota(jnp.int32, (rows, fine), 1)
    spread = (row // 2 == sample).astype(F32)
    for p in range(TAPS):
        wide = jnp.broadcast_to(taps_ref[p : p + 1, :], (TILE, fine))
        taps_wide[p] = lax.dot_general(
            spread, wide, (((1,), (1,)), ((), ())),
            precision=lax.Precision.HIGHEST, preferred_element_type=F32,
        )

    keep = jnp.where(me == count - 1, 0.0, 1.0).astype(F32)
    group = 16
    width = 2 * FRAMES * TILE

    def filter_position(position):
        def filter_rows(step, carry):
            at = pl.ds(pl.multiple_of(step * group, group), group)
            taps = [taps_wide[p, at, :] for p in range(TAPS)]
            for side in range(2):
                series = [own_rows[side * STEPS + position, f, at, :].astype(F32) for f in range(FRAMES)]
                for f in range(FRAMES):
                    mine = taps[0] * series[f]
                    for p in range(1, f + 1):
                        mine = mine + taps[p] * series[f - p]
                    later = taps[f + 1] * series[FRAMES - 1]
                    for p in range(f + 2, TAPS):
                        later = later + taps[p] * series[FRAMES + f - p]
                    to = (side * FRAMES + f) * TILE
                    weighted[position, at, to : to + TILE] = mine.astype(BF16)
                    weighted[position, at, width + to : width + to + TILE] = (later * keep).astype(BF16)
            return carry

        lax.fori_loop(0, rows // group, filter_rows, 0)

    def transform(position, kind, entry, target, added=None):
        rows_at = slice(2 * plane * entry, 2 * plane * entry + near_rows)
        tiles = table_rows.shape[1]
        table = jnp.concatenate(
            [
                jnp.concatenate([table_rows[parity, tile, rows_at, :] for tile in range(tiles)], 1)
                for parity in range(2)
            ], 0,
        )
        for pair in range(FRAMES):
            base = kind * width + 2 * pair * TILE
            sums = jnp.dot(table, weighted[position, :, base : base + 2 * TILE], preferred_element_type=F32)
            for half in range(2):
                side, f = divmod(2 * pair + half, FRAMES)
                for parity in range(2):
                    one = sums[parity * near_rows : (parity + 1) * near_rows, half * TILE : (half + 1) * TILE]
                    if added is not None:
                        one = one + added[position, 1 - kind, side, parity, f].astype(F32)
                    target[position, kind, side, parity, f] = one.astype(BF16)

    def near(position):
        return [
            pltpu.make_async_remote_copy(
                part_send.at[position, kind], part_recv.at[position, kind],
                near_send.at[position, kind], near_recv.at[position, kind],
                device_id={"chan": peer}, device_id_type=MESH,
            )
            for kind, peer in enumerate((down, up))
        ]

    def prepare(position):
        for side in range(2):
            load(position, side).wait()
        filter_position(position)
        if position == 0:
            pltpu.make_async_copy(table_ref, table_ref, const_sem.at[0]).wait()
        transform(position, 0, 0, part_send_rows)
        transform(position, 1, REACH + 1, part_send_rows)

    prepare(0)
    pl.semaphore_wait(barrier, greeted)
    for position in range(STEPS):
        if position:
            prepare(position)
        for copy in near(position):
            copy.start()

    def extent(part):
        first, positions, channel, channels = PARTS[part]
        return pl.ds(first, positions), pl.ds(channel, channels)

    def send_part(part):
        at, channels = extent(part)
        targets = [
            recv.at[at, :, channels, pl.ds(FRAMES * block, FRAMES)] for block in (me, up)
        ]

        def source(kind, away, across):
            entry = away if kind == 0 else REACH - 1 - away
            return send.at[at, kind, :, channels, :, entry * plane + lax.rem(column + across, plane)]

        for kind in range(2):
            pltpu.make_async_copy(source(kind, 0, 0), targets[kind], recv_sem.at[part]).start()

        def turn(index, carry):
            away, across = index // plane, lax.rem(index, plane)
            for kind, way in ((0, 1), (1, -1)):
                pltpu.make_async_remote_copy(
                    source(kind, away, across), targets[kind], send_sem.at[part], recv_sem.at[part],
                    device_id={"chan": chip(way * away, across)}, device_id_type=MESH,
                ).start()
            return carry

        lax.fori_loop(1, REACH * plane, turn, 0)

    for position in range(STEPS):
        for copy in near(position):
            copy.wait_recv()
        transform(position, 0, REACH, send_rows, part_recv_rows)
        transform(position, 1, 1, send_rows, part_recv_rows)
        for part, (first, positions, _, _) in enumerate(PARTS):
            if first + positions - 1 == position:
                send_part(part)
    turn_copy.wait()

    span = min(256, depth)

    def across(part):
        at, channels = extent(part)
        return pltpu.make_async_remote_copy(
            recv.at[at, :, channels], other.at[at, :, channels], core_send.at[part], core_recv.at[part],
            device_id={"tm": 1 - core}, device_id_type=MESH,
        )

    def turn_part(part, source, base):
        first, positions, channel, channels = PARTS[part]

        def turn_block(position, side):
            def one(parity, carry):
                for piece in range(depth // span):
                    flat = source[position, side, parity, piece * span : (piece + 1) * span, :].T
                    to = slice(base + piece * span, base + (piece + 1) * span)
                    left[side * STEPS + position, parity, 0:TILE, to] = flat
                    left[side * STEPS + position, parity, TILE : 2 * TILE, to] = jnp.dot(
                        flat, whole(turn_ref), preferred_element_type=F32
                    ).astype(BF16)
                return carry

            lax.fori_loop(channel, channel + channels, one, 0)

        for position in range(first, first + positions):
            for side in range(2):
                block = BLOCKS[side][position]
                if block == 2:
                    turn_block(position, side)
                else:
                    pl.when(core == (0 if block < 2 else 1))(functools.partial(turn_block, position, side))

    def multiply_part(part, source, base):
        first, positions, channel, channels = PARTS[part]
        total, codes = codes_of(part)

        def one_unit(step, carry):
            a, b, c = (lax.rem(code, 8) for code in carry[:3])
            slots = [lax.rem(code, 32) for code in carry[3:]]
            for parity in range(channel, channel + channels):
                right = jnp.concatenate(
                    [source[lax.rem(at, STEPS), at // STEPS, parity] for at in (b, c)], 1
                )
                sums = jnp.dot(left[a, parity, :, base : base + depth], right, preferred_element_type=F32)
                parts = []
                for index, slot in enumerate(slots):
                    weight = mask_ref[parity, slot + 18 * core].astype(F32) * scale
                    one = sums[:, index * TILE : (index + 1) * TILE].reshape(2, TILE, TILE) * weight
                    parts.append(one + out_ref[slot, parity] if base else one)
                for slot, one in zip(slots, parts):
                    out_ref[slot, parity] = one
            return tuple(code // 8 for code in carry[:3]) + tuple(code // 32 for code in carry[3:])

        start = tuple(low + core * (high - low) for low, high in zip(*codes))
        lax.fori_loop(0, total, one_unit, start, unroll=total if channels == 1 else 1)

    for part in range(len(PARTS)):
        at, channels = extent(part)
        arrived = recv.at[at, :, channels]
        pltpu.make_async_copy(arrived, arrived, recv_sem.at[part]).wait()
        across(part).start()
        turn_part(part, recv_rows, 0)
        multiply_part(part, recv_rows, 0)
        across(part).wait_recv()
        turn_part(part, other_rows, depth)
        multiply_part(part, other_rows, depth)

    for part in range(len(PARTS)):
        at, channels = extent(part)
        sent = send.at[at, :, :, channels, :, pl.ds(0, REACH * plane - 1)]
        pltpu.make_async_copy(sent, sent, send_sem.at[part]).wait()
        across(part).wait_send()
    for position in range(STEPS):
        for copy in near(position):
            copy.wait_send()


def per_device(count, voltages, filter_taps, block_mask):
    fine = 2 * count
    frames = voltages.reshape(FRAMES, fine, 2, NBLK * TILE)
    depth = 2 * FRAMES * count
    span = min(256, depth)
    table, rotation = dft_table(fine), turn_table(span)
    dma = pltpu.SemaphoreType.DMA
    vmem = pl.BlockSpec(memory_space=pltpu.VMEM)
    anywhere = pl.BlockSpec(memory_space=pl.ANY)
    parts = len(PARTS)
    spectra = (STEPS, 2, 2, 2, FRAMES, REACH * (count // RING), 2, TILE)
    return pl.pallas_call(
        functools.partial(kernel, count),
        out_shape=pltpu.VMEM((18, 2, 2, TILE, TILE), F32),
        in_specs=[anywhere, vmem, anywhere, anywhere, pl.BlockSpec(memory_space=pltpu.SMEM)],
        out_specs=vmem,
        scratch_shapes=[
            pltpu.VMEM((NBLK, FRAMES, fine, 2, TILE), BF16),
            pltpu.VMEM((TAPS, 2 * fine, TILE), F32),
            pltpu.VMEM(table.shape[1:3] + ((RING + 1) * (count // RING),) + table.shape[4:], BF16),
            pltpu.VMEM(rotation.shape, BF16),
            pltpu.VMEM((STEPS, 2 * fine, 4 * FRAMES * TILE), BF16),
            pltpu.VMEM(spectra, BF16),
            pltpu.VMEM(spectra, BF16),
            pltpu.VMEM(spectra, BF16),
            pltpu.VMEM((STEPS, 2, 2, FRAMES * count, 2, TILE), BF16),
            pltpu.VMEM((STEPS, 2, 2, FRAMES * count, 2, TILE), BF16),
            pltpu.VMEM((NBLK, 2, 2 * TILE, 2 * depth), BF16),
            dma((NBLK,)), dma((2,)), dma((STEPS, 2)), dma((STEPS, 2)), dma((parts,)), dma((parts,)),
            dma((parts,)), dma((parts,)),
        ],
        compiler_params=pltpu.CompilerParams(
            collective_id=0, has_side_effects=True, vmem_limit_bytes=54 * 2**20
        ),
        cost_estimate=pl.CostEstimate(flops=6 * 10**9, bytes_accessed=10**7, transcendentals=0),
        name="correlate",
    )(frames, filter_taps, table, rotation, block_mask.T)


def solution(mesh):
    in_specs = (P("tm", "chan", None, None, None, None), P(), P(None, "chan"))
    out_specs = P("tm", "chan", None, None, None)
    return jax.shard_map(
        functools.partial(per_device, mesh.shape["chan"]),
        mesh=mesh, in_specs=in_specs, out_specs=out_specs, check_vma=False,
    )
```

```python
import functools
import math

import jax
import jax.numpy as jnp
import numpy as np
from jax import lax
from jax.experimental import pallas as pl
from jax.experimental.pallas import tpu as pltpu
from jax.sharding import PartitionSpec as P

TAPS = 4
FRAMES = 3
TILE = 128
NBLK = 8
STEPS = 4
RING = 8
REACH = 4
MESH = pl.DeviceIdType.MESH
BF16 = jnp.bfloat16
F32 = jnp.float32

PAIRS = [(a, b) for a in range(NBLK) for b in range(a, NBLK)]


def in_tiles(table):
    width = min(TILE, table.shape[-1])
    table = table.reshape(table.shape[:-2] + (table.shape[-2] // 2, 2, table.shape[-1] // width, width))
    return jnp.asarray(np.moveaxis(table, -2, -4).astype(BF16))


def whole(ref, *index):
    flat = merged(ref)
    return jnp.concatenate([flat[index + (tile,)] for tile in range(flat.shape[len(index)])], 1)


def dft_table(size):
    index = np.arange(size)
    angle = (index[:, None] * index[None, :] % size).astype(np.float32) * np.float32(2.0 * math.pi / size)
    cosine = np.cos(angle) / np.float32(math.sqrt(size))
    sine = np.sin(angle) / np.float32(math.sqrt(size))
    upper = np.stack([cosine, sine], 2)
    lower = np.stack([-sine, cosine], 2)
    plane = size // 2 // RING
    table = np.stack([upper, lower], 1).reshape(plane, RING, 2, 2, 2 * size)
    table = np.transpose(table, (1, 2, 0, 3, 4)).reshape(RING, 2, 2 * plane, 2 * size)
    return in_tiles(table)


def turn_table(size):
    turn = np.zeros((size, size), np.float32)
    even = np.arange(0, size, 2)
    turn[even + 1, even] = 1.0
    turn[even, even + 1] = -1.0
    return in_tiles(turn)


BLOCKS = ((0, 1, 3, 2), (5, 6, 7, 4))
PARTS = ((0, 1, 0, 2, 0, 2), (1, 2, 0, 2, 0, 2), (3, 1, 0, 1, 0, 2), (3, 1, 1, 1, 0, 1), (3, 1, 1, 1, 1, 1))


def places_in(part):
    first, positions, side, sides = PARTS[part][:4]
    return {s * STEPS + p for s in range(side, side + sides) for p in range(first, first + positions)}


def place_of(block):
    half = block // STEPS
    return half * STEPS + BLOCKS[half].index(block)


def units_of(part, core):
    fresh = places_in(part)
    ready = set().union(*(places_in(earlier) for earlier in range(part + 1)))
    units = []
    for a in range(NBLK):
        row = []
        for b in range(a, NBLK):
            slot = PAIRS.index((a, b)) - 18 * core
            at = {place_of(a), place_of(b)}
            if 0 <= slot < 18 and at & fresh and at <= ready:
                row.append((b, slot))
        if len(row) % 2:
            row.append(row[-1])
        for (b, slot), (c, other) in zip(row[::2], row[1::2]):
            units.append((place_of(a), place_of(b), place_of(c), slot, other))
    return units


def codes_of(part):
    units = [units_of(part, core) for core in range(2)]
    count = max(len(units[0]), len(units[1]))
    codes = []
    for mine in units:
        while len(mine) < count:
            index = next(i for i, unit in enumerate(mine) if unit[3] != unit[4])
            a, b, c, slot, other = mine[index]
            mine[index : index + 1] = [(a, b, b, slot, slot), (a, c, c, other, other)]
        codes.append([
            sum(unit[field] * base**place for place, unit in enumerate(mine))
            for field, base in enumerate((8, 8, 8, 32, 32))
        ])
    return count, codes


def merged(ref):
    shape = ref.shape
    return ref.reshape(shape[:-3] + (shape[-3] * shape[-2], shape[-1]))


def kernel(
    count,
    v_ref, taps_ref, table_hbm, turn_hbm, mask_ref, out_ref,
    own, taps_wide, table_ref, turn_ref, weighted, part_send, part_recv, send, recv, other, left,
    load_sem, const_sem, near_send, near_recv, send_sem, recv_sem, core_send, core_recv, met_sem,
):
    me = lax.axis_index("chan")
    core = lax.axis_index("tm")
    fine = 2 * count
    rows = 2 * fine
    depth = 2 * FRAMES * count
    plane = count // RING
    near_rows = 2 * REACH * plane
    here = lax.rem(me, RING)
    column = me // RING
    up = lax.rem(me + 1, count)
    down = lax.rem(me + count - 1, count)
    scale = 1.0 / math.sqrt(FRAMES * count * 2)

    own_rows, table_rows = merged(own), merged(table_ref)
    part_send_rows, part_recv_rows = merged(part_send), merged(part_recv)
    send_rows, recv_rows, other_rows = merged(send), merged(recv), merged(other)

    def load(position, side):
        block = BLOCKS[side][position]
        index = side * STEPS + position
        lanes = pl.ds(block * TILE, TILE)
        return pltpu.make_async_copy(v_ref.at[:, :, :, lanes], own.at[index], load_sem.at[index])

    for position in range(STEPS):
        for side in range(2):
            load(position, side).start()
    for entry in range(RING + 1):
        pltpu.make_async_copy(
            table_hbm.at[lax.rem(here + entry + RING - REACH, RING)],
            table_ref.at[:, :, pl.ds(entry * plane, plane)], const_sem.at[0],
        ).start()
    turn_copy = pltpu.make_async_copy(turn_hbm, turn_ref, const_sem.at[1])
    turn_copy.start()

    def chip(along, across):
        return lax.rem(column + across, plane) * RING + lax.rem(here + along + RING, RING)

    barrier = pltpu.get_barrier_semaphore()

    def tell_group(semaphore):
        def tell(along, across):
            peer = chip(along, across)
            pl.semaphore_signal(semaphore, inc=1, device_id={"chan": peer}, device_id_type=MESH)

        def tell_ring(index, carry):
            tell(index, 0)
            return carry

        def tell_plane(index, carry):
            tell(0, index)
            return carry

        lax.fori_loop(1, RING, tell_ring, 0)
        lax.fori_loop(1, plane, tell_plane, 0)

    group_size = RING - 1 + plane - 1
    for peer in (up, down):
        pl.semaphore_signal(barrier, inc=1, device_id={"chan": peer}, device_id_type=MESH)
    pl.semaphore_signal(barrier, inc=1, device_id={"tm": 1 - core}, device_id_type=MESH)
    tell_group(barrier)

    row = lax.broadcasted_iota(jnp.int32, (rows, fine), 0)
    sample = lax.broadcasted_iota(jnp.int32, (rows, fine), 1)
    spread = (row // 2 == sample).astype(F32)
    for p in range(TAPS):
        wide = jnp.broadcast_to(taps_ref[p : p + 1, :], (TILE, fine))
        taps_wide[p] = lax.dot_general(
            spread, wide, (((1,), (1,)), ((), ())),
            precision=lax.Precision.HIGHEST, preferred_element_type=F32,
        )

    keep = jnp.where(me == count - 1, 0.0, 1.0).astype(F32)
    group = 16
    width = 2 * FRAMES * TILE

    def filter_position(position):
        def filter_rows(step, carry):
            at = pl.ds(pl.multiple_of(step * group, group), group)
            taps = [taps_wide[p, at, :] for p in range(TAPS)]
            for side in range(2):
                series = [own_rows[side * STEPS + position, f, at, :].astype(F32) for f in range(FRAMES)]
                for f in range(FRAMES):
                    mine = taps[0] * series[f]
                    for p in range(1, f + 1):
                        mine = mine + taps[p] * series[f - p]
                    later = taps[f + 1] * series[FRAMES - 1]
                    for p in range(f + 2, TAPS):
                        later = later + taps[p] * series[FRAMES + f - p]
                    to = (side * FRAMES + f) * TILE
                    weighted[position, at, to : to + TILE] = mine.astype(BF16)
                    weighted[position, at, width + to : width + to + TILE] = (later * keep).astype(BF16)
            return carry

        lax.fori_loop(0, rows // group, filter_rows, 0)

    def transform(position, kind, entry, target, added=None):
        rows_at = slice(2 * plane * entry, 2 * plane * entry + near_rows)
        tiles = table_rows.shape[1]
        table = jnp.concatenate(
            [
                jnp.concatenate([table_rows[parity, tile, rows_at, :] for tile in range(tiles)], 1)
                for parity in range(2)
            ], 0,
        )
        for pair in range(FRAMES):
            base = kind * width + 2 * pair * TILE
            sums = jnp.dot(table, weighted[position, :, base : base + 2 * TILE], preferred_element_type=F32)
            for half in range(2):
                side, f = divmod(2 * pair + half, FRAMES)
                for parity in range(2):
                    one = sums[parity * near_rows : (parity + 1) * near_rows, half * TILE : (half + 1) * TILE]
                    if added is not None:
                        one = one + added[position, 1 - kind, side, parity, f].astype(F32)
                    target[position, kind, side, parity, f] = one.astype(BF16)

    def near(position):
        return [
            pltpu.make_async_remote_copy(
                part_send.at[position, kind], part_recv.at[position, kind],
                near_send.at[position, kind], near_recv.at[position, kind],
                device_id={"chan": peer}, device_id_type=MESH,
            )
            for kind, peer in enumerate((down, up))
        ]

    def prepare(position):
        for side in range(2):
            load(position, side).wait()
        filter_position(position)
        if position == 0:
            pltpu.make_async_copy(table_ref, table_ref, const_sem.at[0]).wait()
        transform(position, 0, 0, part_send_rows)
        transform(position, 1, REACH + 1, part_send_rows)

    prepare(0)
    pl.semaphore_wait(barrier, group_size + 3)
    for position in range(STEPS):
        if position:
            prepare(position)
        for copy in near(position):
            copy.start()
        if position == 0:
            tell_group(met_sem)

    def extent(part):
        first, positions, side, sides, channel, channels = PARTS[part]
        return pl.ds(first, positions), pl.ds(side, sides), pl.ds(channel, channels)

    def send_part(part):
        at, sides, channels = extent(part)
        targets = [
            recv.at[at, sides, channels, pl.ds(FRAMES * block, FRAMES)] for block in (me, up)
        ]

        def source(kind, away, across):
            entry = away if kind == 0 else REACH - 1 - away
            return send.at[at, kind, sides, channels, :, entry * plane + lax.rem(column + across, plane)]

        for kind in range(2):
            pltpu.make_async_copy(source(kind, 0, 0), targets[kind], recv_sem.at[part]).start()

        def turn(index, carry):
            away, across = index // plane, lax.rem(index, plane)
            for kind, way in ((0, 1), (1, -1)):
                pltpu.make_async_remote_copy(
                    source(kind, away, across), targets[kind], send_sem.at[part], recv_sem.at[part],
                    device_id={"chan": chip(way * away, across)}, device_id_type=MESH,
                ).start()
            return carry

        lax.fori_loop(1, REACH * plane, turn, 0)

    for position in range(STEPS):
        for copy in near(position):
            copy.wait_recv()
        if position == 0:
            pl.semaphore_wait(met_sem, group_size)
        transform(position, 0, REACH, send_rows, part_recv_rows)
        transform(position, 1, 1, send_rows, part_recv_rows)
        for part in range(len(PARTS)):
            if PARTS[part][0] + PARTS[part][1] - 1 == position:
                send_part(part)
    turn_copy.wait()

    span = min(256, depth)

    def across(part):
        at, sides, channels = extent(part)
        return pltpu.make_async_remote_copy(
            recv.at[at, sides, channels], other.at[at, sides, channels], core_send.at[part], core_recv.at[part],
            device_id={"tm": 1 - core}, device_id_type=MESH,
        )

    def turn_part(part, source, base):
        first, positions, first_side, sides, channel, channels = PARTS[part]

        def turn_block(position, side):
            def one(parity, carry):
                for piece in range(depth // span):
                    flat = source[position, side, parity, piece * span : (piece + 1) * span, :].T
                    to = slice(base + piece * span, base + (piece + 1) * span)
                    left[side * STEPS + position, parity, 0:TILE, to] = flat
                    left[side * STEPS + position, parity, TILE : 2 * TILE, to] = jnp.dot(
                        flat, whole(turn_ref), preferred_element_type=F32
                    ).astype(BF16)
                return carry

            lax.fori_loop(channel, channel + channels, one, 0)

        for position in range(first, first + positions):
            for side in range(first_side, first_side + sides):
                block = BLOCKS[side][position]
                if block == 2:
                    turn_block(position, side)
                else:
                    pl.when(core == (0 if block < 2 else 1))(functools.partial(turn_block, position, side))

    def multiply_part(part, source, base):
        channel, channels = PARTS[part][4:]
        total, codes = codes_of(part)

        def one_unit(step, carry):
            a, b, c = (lax.rem(code, 8) for code in carry[:3])
            slots = [lax.rem(code, 32) for code in carry[3:]]
            for parity in range(channel, channel + channels):
                right = jnp.concatenate(
                    [source[lax.rem(at, STEPS), at // STEPS, parity] for at in (b, c)], 1
                )
                sums = jnp.dot(left[a, parity, :, base : base + depth], right, preferred_element_type=F32)
                parts = []
                for index, slot in enumerate(slots):
                    weight = mask_ref[parity, slot + 18 * core].astype(F32) * scale
                    one = sums[:, index * TILE : (index + 1) * TILE].reshape(2, TILE, TILE) * weight
                    parts.append(one + out_ref[slot, parity] if base else one)
                for slot, one in zip(slots, parts):
                    out_ref[slot, parity] = one
            return tuple(code // 8 for code in carry[:3]) + tuple(code // 32 for code in carry[3:])

        start = tuple(low + core * (high - low) for low, high in zip(*codes))
        lax.fori_loop(0, total, one_unit, start, unroll=total if channels == 1 else 1)

    for part in range(len(PARTS)):
        at, sides, channels = extent(part)
        arrived = recv.at[at, sides, channels]
        pltpu.make_async_copy(arrived, arrived, recv_sem.at[part]).wait()
        across(part).start()
        turn_part(part, recv_rows, 0)
        multiply_part(part, recv_rows, 0)
        across(part).wait_recv()
        turn_part(part, other_rows, depth)
        multiply_part(part, other_rows, depth)

    for part in range(len(PARTS)):
        at, sides, channels = extent(part)
        sent = send.at[at, :, sides, channels, :, pl.ds(0, REACH * plane - 1)]
        pltpu.make_async_copy(sent, sent, send_sem.at[part]).wait()
        across(part).wait_send()
    for position in range(STEPS):
        for copy in near(position):
            copy.wait_send()


def per_device(count, voltages, filter_taps, block_mask):
    fine = 2 * count
    frames = voltages.reshape(FRAMES, fine, 2, NBLK * TILE)
    depth = 2 * FRAMES * count
    span = min(256, depth)
    table, rotation = dft_table(fine), turn_table(span)
    dma = pltpu.SemaphoreType.DMA
    vmem = pl.BlockSpec(memory_space=pltpu.VMEM)
    anywhere = pl.BlockSpec(memory_space=pl.ANY)
    parts = len(PARTS)
    spectra = (STEPS, 2, 2, 2, FRAMES, REACH * (count // RING), 2, TILE)
    return pl.pallas_call(
        functools.partial(kernel, count),
        out_shape=pltpu.VMEM((18, 2, 2, TILE, TILE), F32),
        in_specs=[anywhere, vmem, anywhere, anywhere, pl.BlockSpec(memory_space=pltpu.SMEM)],
        out_specs=vmem,
        scratch_shapes=[
            pltpu.VMEM((NBLK, FRAMES, fine, 2, TILE), BF16),
            pltpu.VMEM((TAPS, 2 * fine, TILE), F32),
            pltpu.VMEM(table.shape[1:3] + ((RING + 1) * (count // RING),) + table.shape[4:], BF16),
            pltpu.VMEM(rotation.shape, BF16),
            pltpu.VMEM((STEPS, 2 * fine, 4 * FRAMES * TILE), BF16),
            pltpu.VMEM(spectra, BF16),
            pltpu.VMEM(spectra, BF16),
            pltpu.VMEM(spectra, BF16),
            pltpu.VMEM((STEPS, 2, 2, FRAMES * count, 2, TILE), BF16),
            pltpu.VMEM((STEPS, 2, 2, FRAMES * count, 2, TILE), BF16),
            pltpu.VMEM((NBLK, 2, 2 * TILE, 2 * depth), BF16),
            dma((NBLK,)), dma((2,)), dma((STEPS, 2)), dma((STEPS, 2)), dma((parts,)), dma((parts,)),
            dma((parts,)), dma((parts,)), pltpu.SemaphoreType.REGULAR,
        ],
        compiler_params=pltpu.CompilerParams(
            collective_id=0, has_side_effects=True, vmem_limit_bytes=54 * 2**20
        ),
        cost_estimate=pl.CostEstimate(flops=6 * 10**9, bytes_accessed=10**7, transcendentals=0),
        name="correlate",
    )(frames, filter_taps, table, rotation, block_mask.T)


def solution(mesh):
    in_specs = (P("tm", "chan", None, None, None, None), P(), P(None, "chan"))
    out_specs = P("tm", "chan", None, None, None)
    return jax.shard_map(
        functools.partial(per_device, mesh.shape["chan"]),
        mesh=mesh, in_specs=in_specs, out_specs=out_specs, check_vma=False,
    )
```

```python
import functools
import math

import jax
import jax.numpy as jnp
import numpy as np
from jax import lax
from jax.experimental import pallas as pl
from jax.experimental.pallas import tpu as pltpu
from jax.sharding import PartitionSpec as P

TAPS = 4
FRAMES = 3
TILE = 128
NBLK = 8
STEPS = 4
RING = 8
REACH = 4
MESH = pl.DeviceIdType.MESH
BF16 = jnp.bfloat16
F32 = jnp.float32

PAIRS = [(a, b) for a in range(NBLK) for b in range(a, NBLK)]


def in_tiles(table):
    width = min(TILE, table.shape[-1])
    table = table.reshape(table.shape[:-2] + (table.shape[-2] // 2, 2, table.shape[-1] // width, width))
    return jnp.asarray(np.moveaxis(table, -2, -4).astype(BF16))


def whole(ref, *index):
    flat = merged(ref)
    return jnp.concatenate([flat[index + (tile,)] for tile in range(flat.shape[len(index)])], 1)


def dft_table(size):
    index = np.arange(size)
    angle = (index[:, None] * index[None, :] % size).astype(np.float32) * np.float32(2.0 * math.pi / size)
    cosine = np.cos(angle) / np.float32(math.sqrt(size))
    sine = np.sin(angle) / np.float32(math.sqrt(size))
    upper = np.stack([cosine, sine], 2)
    lower = np.stack([-sine, cosine], 2)
    plane = size // 2 // RING
    table = np.stack([upper, lower], 1).reshape(plane, RING, 2, 2, 2 * size)
    table = np.transpose(table, (2, 1, 0, 3, 4))
    table = np.concatenate([table, table], 1).reshape(2, 4 * RING * plane, 2 * size)
    return in_tiles(table)


def turn_table(size):
    turn = np.zeros((size, size), np.float32)
    even = np.arange(0, size, 2)
    turn[even + 1, even] = 1.0
    turn[even, even + 1] = -1.0
    return in_tiles(turn)


BLOCKS = ((0, 3, 1, 2), (5, 7, 6, 4))
PARTS = ((0, 1, 0, 2, 0, 2), (1, 1, 0, 2, 0, 2), (2, 1, 0, 2, 0, 2), (3, 1, 0, 1, 0, 2), (3, 1, 1, 1, 0, 1), (3, 1, 1, 1, 1, 1))


def places_in(part):
    first, positions, side, sides = PARTS[part][:4]
    return {s * STEPS + p for s in range(side, side + sides) for p in range(first, first + positions)}


def place_of(block):
    half = block // STEPS
    return half * STEPS + BLOCKS[half].index(block)


def units_of(part, core):
    fresh = places_in(part)
    ready = set().union(*(places_in(earlier) for earlier in range(part + 1)))
    units = []
    for a in range(NBLK):
        row = []
        for b in range(a, NBLK):
            slot = PAIRS.index((a, b)) - 18 * core
            at = {place_of(a), place_of(b)}
            if 0 <= slot < 18 and at & fresh and at <= ready:
                row.append((b, slot))
        if len(row) % 2:
            row.append(row[-1])
        for (b, slot), (c, other) in zip(row[::2], row[1::2]):
            units.append((place_of(a), place_of(b), place_of(c), slot, other))
    return units


def codes_of(part):
    units = [units_of(part, core) for core in range(2)]
    count = max(len(units[0]), len(units[1]))
    codes = []
    for mine in units:
        while len(mine) < count:
            index = next((i for i, unit in enumerate(mine) if unit[3] != unit[4]), None)
            if index is None:
                break
            a, b, c, slot, other = mine[index]
            mine[index : index + 1] = [(a, b, b, slot, slot), (a, c, c, other, other)]
        codes.append([
            sum(unit[field] * base**place for place, unit in enumerate(mine))
            for field, base in enumerate((8, 8, 8, 32, 32))
        ])
    return [len(mine) for mine in units], codes


def merged(ref):
    shape = ref.shape
    return ref.reshape(shape[:-3] + (shape[-3] * shape[-2], shape[-1]))


def kernel(
    count,
    v_ref, taps_ref, table_hbm, turn_hbm, mask_ref, out_ref,
    own, taps_wide, table_ref, turn_ref, weighted, part_send, part_recv, send, recv, other, left,
    load_sem, const_sem, near_send, near_recv, send_sem, recv_sem, core_send, core_recv, met_sem,
):
    me = lax.axis_index("chan")
    core = lax.axis_index("tm")
    fine = 2 * count
    rows = 2 * fine
    depth = 2 * FRAMES * count
    plane = count // RING
    near_rows = 2 * REACH * plane
    here = lax.rem(me, RING)
    column = me // RING
    up = lax.rem(me + 1, count)
    down = lax.rem(me + count - 1, count)
    scale = 1.0 / math.sqrt(FRAMES * count * 2)

    own_rows, table_rows = merged(own), merged(table_ref)
    part_send_rows, part_recv_rows = merged(part_send), merged(part_recv)
    send_rows, recv_rows, other_rows = merged(send), merged(recv), merged(other)

    def load(position, side):
        block = BLOCKS[side][position]
        index = side * STEPS + position
        lanes = pl.ds(block * TILE, TILE)
        return pltpu.make_async_copy(v_ref.at[:, :, :, lanes], own.at[index], load_sem.at[index])

    entries = (RING + 1) * plane
    first_entry = lax.rem(here + RING - REACH, RING) * plane
    table_copy = pltpu.make_async_copy(
        table_hbm.at[:, :, pl.ds(first_entry, entries)], table_ref, const_sem.at[0]
    )
    turn_copy = pltpu.make_async_copy(turn_hbm, turn_ref, const_sem.at[1])
    for side in range(2):
        load(0, side).start()
    table_copy.start()

    def chip(along, across):
        return lax.rem(column + across, plane) * RING + lax.rem(here + along + RING, RING)

    barrier = pltpu.get_barrier_semaphore()

    def tell_group(semaphore):
        def tell(along, across):
            peer = chip(along, across)
            pl.semaphore_signal(semaphore, inc=1, device_id={"chan": peer}, device_id_type=MESH)

        def tell_ring(index, carry):
            tell(index, 0)
            return carry

        def tell_plane(index, carry):
            tell(0, index)
            return carry

        lax.fori_loop(1, RING, tell_ring, 0)
        lax.fori_loop(1, plane, tell_plane, 0)

    group_size = RING - 1 + plane - 1
    for peer in (up, down):
        pl.semaphore_signal(barrier, inc=1, device_id={"chan": peer}, device_id_type=MESH)
    pl.semaphore_signal(barrier, inc=1, device_id={"tm": 1 - core}, device_id_type=MESH)
    tell_group(barrier)
    for position in range(1, STEPS):
        for side in range(2):
            load(position, side).start()
    turn_copy.start()

    row = lax.broadcasted_iota(jnp.int32, (rows, fine), 0)
    sample = lax.broadcasted_iota(jnp.int32, (rows, fine), 1)
    spread = (row // 2 == sample).astype(F32)
    for p in range(TAPS):
        wide = jnp.broadcast_to(taps_ref[p : p + 1, :], (TILE, fine))
        taps_wide[p] = lax.dot_general(
            spread, wide, (((1,), (1,)), ((), ())),
            precision=lax.Precision.HIGHEST, preferred_element_type=F32,
        )

    keep = jnp.where(me == count - 1, 0.0, 1.0).astype(F32)
    group = 16
    width = 2 * FRAMES * TILE

    def filter_position(position):
        def filter_rows(step, carry):
            at = pl.ds(pl.multiple_of(step * group, group), group)
            taps = [taps_wide[p, at, :] for p in range(TAPS)]
            for side in range(2):
                series = [own_rows[side * STEPS + position, f, at, :].astype(F32) for f in range(FRAMES)]
                for f in range(FRAMES):
                    mine = taps[0] * series[f]
                    for p in range(1, f + 1):
                        mine = mine + taps[p] * series[f - p]
                    later = taps[f + 1] * series[FRAMES - 1]
                    for p in range(f + 2, TAPS):
                        later = later + taps[p] * series[FRAMES + f - p]
                    to = (side * FRAMES + f) * TILE
                    weighted[position, at, to : to + TILE] = mine.astype(BF16)
                    weighted[position, at, width + to : width + to + TILE] = (later * keep).astype(BF16)
            return carry

        lax.fori_loop(0, rows // group, filter_rows, 0)

    def transform(position, kind, entry, target, added=None):
        rows_at = slice(2 * plane * entry, 2 * plane * entry + near_rows)
        tiles = table_rows.shape[1]
        table = jnp.concatenate(
            [
                jnp.concatenate([table_rows[parity, tile, rows_at, :] for tile in range(tiles)], 1)
                for parity in range(2)
            ], 0,
        )
        for pair in range(FRAMES):
            base = kind * width + 2 * pair * TILE
            sums = jnp.dot(table, weighted[position, :, base : base + 2 * TILE], preferred_element_type=F32)
            for half in range(2):
                side, f = divmod(2 * pair + half, FRAMES)
                for parity in range(2):
                    one = sums[parity * near_rows : (parity + 1) * near_rows, half * TILE : (half + 1) * TILE]
                    if added is not None:
                        one = one + added[position, 1 - kind, side, parity, f].astype(F32)
                    target[position, kind, side, parity, f] = one.astype(BF16)

    def near(position):
        return [
            pltpu.make_async_remote_copy(
                part_send.at[position, kind], part_recv.at[position, kind],
                near_send.at[position, kind], near_recv.at[position, kind],
                device_id={"chan": peer}, device_id_type=MESH,
            )
            for kind, peer in enumerate((down, up))
        ]

    def prepare(position):
        for side in range(2):
            load(position, side).wait()
        filter_position(position)
        if position == 0:
            table_copy.wait()
        transform(position, 0, 0, part_send_rows)
        transform(position, 1, REACH + 1, part_send_rows)

    prepare(0)
    pl.semaphore_wait(barrier, group_size + 3)
    for position in range(STEPS):
        if position:
            prepare(position)
        for copy in near(position):
            copy.start()
        if position == 0:
            tell_group(met_sem)

    def extent(part):
        first, positions, side, sides, channel, channels = PARTS[part]
        return pl.ds(first, positions), pl.ds(side, sides), pl.ds(channel, channels)

    def send_part(part):
        at, sides, channels = extent(part)
        targets = [
            recv.at[at, sides, channels, pl.ds(FRAMES * block, FRAMES)] for block in (me, up)
        ]

        def source(kind, away, across):
            entry = away if kind == 0 else REACH - 1 - away
            return send.at[at, kind, sides, channels, :, entry * plane + lax.rem(column + across, plane)]

        for kind in range(2):
            pltpu.make_async_copy(source(kind, 0, 0), targets[kind], recv_sem.at[part]).start()

        def turn(index, carry):
            away, across = index // plane, lax.rem(index, plane)
            for kind, way in ((0, 1), (1, -1)):
                pltpu.make_async_remote_copy(
                    source(kind, away, across), targets[kind], send_sem.at[part], recv_sem.at[part],
                    device_id={"chan": chip(way * away, across)}, device_id_type=MESH,
                ).start()
            return carry

        lax.fori_loop(1, REACH * plane, turn, 0)

    for position in range(STEPS):
        for copy in near(position):
            copy.wait_recv()
        if position == 0:
            pl.semaphore_wait(met_sem, group_size)
        transform(position, 0, REACH, send_rows, part_recv_rows)
        transform(position, 1, 1, send_rows, part_recv_rows)
        for part in range(len(PARTS)):
            if PARTS[part][0] + PARTS[part][1] - 1 == position:
                send_part(part)
    turn_copy.wait()

    span = min(256, depth)

    def across(part):
        at, sides, channels = extent(part)
        return pltpu.make_async_remote_copy(
            recv.at[at, sides, channels], other.at[at, sides, channels], core_send.at[part], core_recv.at[part],
            device_id={"tm": 1 - core}, device_id_type=MESH,
        )

    def turn_part(part, source, base):
        first, positions, first_side, sides, channel, channels = PARTS[part]

        def turn_block(position, side):
            def one(parity, carry):
                for piece in range(depth // span):
                    flat = source[position, side, parity, piece * span : (piece + 1) * span, :].T
                    to = slice(base + piece * span, base + (piece + 1) * span)
                    left[side * STEPS + position, parity, 0:TILE, to] = flat
                    left[side * STEPS + position, parity, TILE : 2 * TILE, to] = jnp.dot(
                        flat, whole(turn_ref), preferred_element_type=F32
                    ).astype(BF16)
                return carry

            lax.fori_loop(channel, channel + channels, one, 0)

        for position in range(first, first + positions):
            for side in range(first_side, first_side + sides):
                block = BLOCKS[side][position]
                if block == 2:
                    turn_block(position, side)
                else:
                    pl.when(core == (0 if block < 2 else 1))(functools.partial(turn_block, position, side))

    def multiply_part(part, source, base):
        channel, channels = PARTS[part][4:]
        (total, other_total), codes = codes_of(part)

        def one_unit(step, carry):
            a, b, c = (lax.rem(code, 8) for code in carry[:3])
            slots = [lax.rem(code, 32) for code in carry[3:]]
            for parity in range(channel, channel + channels):
                right = jnp.concatenate(
                    [source[lax.rem(at, STEPS), at // STEPS, parity] for at in (b, c)], 1
                )
                sums = jnp.dot(left[a, parity, :, base : base + depth], right, preferred_element_type=F32)
                parts = []
                for index, slot in enumerate(slots):
                    weight = mask_ref[parity, slot + 18 * core].astype(F32) * scale
                    one = sums[:, index * TILE : (index + 1) * TILE].reshape(2, TILE, TILE) * weight
                    parts.append(one + out_ref[slot, parity] if base else one)
                for slot, one in zip(slots, parts):
                    out_ref[slot, parity] = one
            return tuple(code // 8 for code in carry[:3]) + tuple(code // 32 for code in carry[3:])

        start = tuple(low + core * (high - low) for low, high in zip(*codes))
        if total == other_total:
            lax.fori_loop(0, total, one_unit, start, unroll=total if channels == 1 else 1)
        else:
            lax.fori_loop(0, total + core * (other_total - total), one_unit, start)

    def finish(part):
        across(part).wait_recv()
        turn_part(part, other_rows, depth)
        multiply_part(part, other_rows, depth)

    for part in range(len(PARTS)):
        at, sides, channels = extent(part)
        arrived = recv.at[at, sides, channels]
        pltpu.make_async_copy(arrived, arrived, recv_sem.at[part]).wait()
        across(part).start()
        if part:
            finish(part - 1)
        turn_part(part, recv_rows, 0)
        multiply_part(part, recv_rows, 0)
    finish(len(PARTS) - 1)

    for part in range(len(PARTS)):
        at, sides, channels = extent(part)
        sent = send.at[at, :, sides, channels, :, pl.ds(0, REACH * plane - 1)]
        pltpu.make_async_copy(sent, sent, send_sem.at[part]).wait()
        across(part).wait_send()
    for position in range(STEPS):
        for copy in near(position):
            copy.wait_send()


def per_device(count, voltages, filter_taps, block_mask):
    fine = 2 * count
    frames = voltages.reshape(FRAMES, fine, 2, NBLK * TILE)
    depth = 2 * FRAMES * count
    span = min(256, depth)
    table, rotation = dft_table(fine), turn_table(span)
    dma = pltpu.SemaphoreType.DMA
    vmem = pl.BlockSpec(memory_space=pltpu.VMEM)
    anywhere = pl.BlockSpec(memory_space=pl.ANY)
    parts = len(PARTS)
    spectra = (STEPS, 2, 2, 2, FRAMES, REACH * (count // RING), 2, TILE)
    return pl.pallas_call(
        functools.partial(kernel, count),
        out_shape=pltpu.VMEM((18, 2, 2, TILE, TILE), F32),
        in_specs=[anywhere, vmem, anywhere, anywhere, pl.BlockSpec(memory_space=pltpu.SMEM)],
        out_specs=vmem,
        scratch_shapes=[
            pltpu.VMEM((NBLK, FRAMES, fine, 2, TILE), BF16),
            pltpu.VMEM((TAPS, 2 * fine, TILE), F32),
            pltpu.VMEM(table.shape[:2] + ((RING + 1) * (count // RING),) + table.shape[3:], BF16),
            pltpu.VMEM(rotation.shape, BF16),
            pltpu.VMEM((STEPS, 2 * fine, 4 * FRAMES * TILE), BF16),
            pltpu.VMEM(spectra, BF16),
            pltpu.VMEM(spectra, BF16),
            pltpu.VMEM(spectra, BF16),
            pltpu.VMEM((STEPS, 2, 2, FRAMES * count, 2, TILE), BF16),
            pltpu.VMEM((STEPS, 2, 2, FRAMES * count, 2, TILE), BF16),
            pltpu.VMEM((NBLK, 2, 2 * TILE, 2 * depth), BF16),
            dma((NBLK,)), dma((2,)), dma((STEPS, 2)), dma((STEPS, 2)), dma((parts,)), dma((parts,)),
            dma((parts,)), dma((parts,)), pltpu.SemaphoreType.REGULAR,
        ],
        compiler_params=pltpu.CompilerParams(
            collective_id=0, has_side_effects=True, vmem_limit_bytes=54 * 2**20
        ),
        cost_estimate=pl.CostEstimate(flops=6 * 10**9, bytes_accessed=10**7, transcendentals=0),
        name="correlate",
    )(frames, filter_taps, table, rotation, block_mask.T)


def solution(mesh):
    in_specs = (P("tm", "chan", None, None, None, None), P(), P(None, "chan"))
    out_specs = P("tm", "chan", None, None, None)
    return jax.shard_map(
        functools.partial(per_device, mesh.shape["chan"]),
        mesh=mesh, in_specs=in_specs, out_specs=out_specs, check_vma=False,
    )
```

```python
import functools
import math

import jax
import jax.numpy as jnp
import numpy as np
from jax import lax
from jax.experimental import pallas as pl
from jax.experimental.pallas import tpu as pltpu
from jax.sharding import PartitionSpec as P

TAPS = 4
FRAMES = 3
TILE = 128
NBLK = 8
STEPS = 4
RING = 8
REACH = 4
MESH = pl.DeviceIdType.MESH
BF16 = jnp.bfloat16
F32 = jnp.float32

PAIRS = [(a, b) for a in range(NBLK) for b in range(a, NBLK)]


def in_tiles(table):
    width = min(TILE, table.shape[-1])
    table = table.reshape(table.shape[:-2] + (table.shape[-2] // 2, 2, table.shape[-1] // width, width))
    return jnp.asarray(np.moveaxis(table, -2, -4).astype(BF16))


def whole(ref, *index):
    flat = merged(ref)
    return jnp.concatenate([flat[index + (tile,)] for tile in range(flat.shape[len(index)])], 1)


def dft_table(size):
    index = np.arange(size)
    angle = (index[:, None] * index[None, :] % size).astype(np.float32) * np.float32(2.0 * math.pi / size)
    cosine = np.cos(angle) / np.float32(math.sqrt(size))
    sine = np.sin(angle) / np.float32(math.sqrt(size))
    upper = np.stack([cosine, sine], 2)
    lower = np.stack([-sine, cosine], 2)
    plane = size // 2 // RING
    table = np.stack([upper, lower], 1).reshape(plane, RING, 2, 2, 2 * size)
    table = np.transpose(table, (2, 1, 0, 3, 4))
    table = np.concatenate([table, table], 1).reshape(2, 4 * RING * plane, 2 * size)
    return in_tiles(table)


def turn_table(size):
    turn = np.zeros((size, size), np.float32)
    even = np.arange(0, size, 2)
    turn[even + 1, even] = 1.0
    turn[even, even + 1] = -1.0
    return in_tiles(turn)


BLOCKS = ((0, 1, 3, 2), (5, 6, 7, 4))
PARTS = ((0, 1, 0, 2, 0, 2), (1, 2, 0, 2, 0, 2), (3, 1, 0, 1, 0, 2), (3, 1, 1, 1, 0, 2))


def places_in(part):
    first, positions, side, sides = PARTS[part][:4]
    return {s * STEPS + p for s in range(side, side + sides) for p in range(first, first + positions)}


def place_of(block):
    half = block // STEPS
    return half * STEPS + BLOCKS[half].index(block)


def units_of(part, core):
    fresh = places_in(part)
    ready = set().union(*(places_in(earlier) for earlier in range(part + 1)))
    units = []
    for a in range(NBLK):
        row = []
        for b in range(a, NBLK):
            slot = PAIRS.index((a, b)) - 18 * core
            at = {place_of(a), place_of(b)}
            if 0 <= slot < 18 and at & fresh and at <= ready:
                row.append((b, slot))
        if len(row) % 2:
            row.append(row[-1])
        for (b, slot), (c, other) in zip(row[::2], row[1::2]):
            units.append((place_of(a), place_of(b), place_of(c), slot, other))
    return units


def codes_of(part):
    units = [units_of(part, core) for core in range(2)]
    count = max(len(units[0]), len(units[1]))
    codes = []
    for mine in units:
        while len(mine) < count:
            index = next((i for i, unit in enumerate(mine) if unit[3] != unit[4]), None)
            if index is None:
                break
            a, b, c, slot, other = mine[index]
            mine[index : index + 1] = [(a, b, b, slot, slot), (a, c, c, other, other)]
        codes.append([
            sum(unit[field] * base**place for place, unit in enumerate(mine))
            for field, base in enumerate((8, 8, 8, 32, 32))
        ])
    return [len(mine) for mine in units], codes


def merged(ref):
    shape = ref.shape
    return ref.reshape(shape[:-3] + (shape[-3] * shape[-2], shape[-1]))


def kernel(
    count,
    v_ref, taps_ref, table_hbm, turn_hbm, mask_ref, out_ref,
    own, taps_wide, table_ref, turn_ref, weighted, part_send, part_recv, send, recv, other, left,
    load_sem, const_sem, near_send, near_recv, send_sem, recv_sem, core_send, core_recv, met_sem,
):
    me = lax.axis_index("chan")
    core = lax.axis_index("tm")
    fine = 2 * count
    rows = 2 * fine
    depth = 2 * FRAMES * count
    plane = count // RING
    near_rows = 2 * REACH * plane
    here = lax.rem(me, RING)
    column = me // RING
    up = lax.rem(me + 1, count)
    down = lax.rem(me + count - 1, count)
    scale = 1.0 / math.sqrt(FRAMES * count * 2)

    own_rows, table_rows = merged(own), merged(table_ref)
    part_send_rows, part_recv_rows = merged(part_send), merged(part_recv)
    send_rows, recv_rows, other_rows = merged(send), merged(recv), merged(other)

    def load(position, side):
        block = BLOCKS[side][position]
        index = side * STEPS + position
        lanes = pl.ds(block * TILE, TILE)
        return pltpu.make_async_copy(v_ref.at[:, :, :, lanes], own.at[index], load_sem.at[index])

    entries = (RING + 1) * plane
    first_entry = lax.rem(here + RING - REACH, RING) * plane
    table_copy = pltpu.make_async_copy(
        table_hbm.at[:, :, pl.ds(first_entry, entries)], table_ref, const_sem.at[0]
    )
    turn_copy = pltpu.make_async_copy(turn_hbm, turn_ref, const_sem.at[1])
    for side in range(2):
        load(0, side).start()
    table_copy.start()

    def chip(along, across):
        return lax.rem(column + across, plane) * RING + lax.rem(here + along + RING, RING)

    barrier = pltpu.get_barrier_semaphore()

    def tell_group(semaphore):
        def tell(along, across):
            peer = chip(along, across)
            pl.semaphore_signal(semaphore, inc=1, device_id={"chan": peer}, device_id_type=MESH)

        def tell_ring(index, carry):
            tell(index, 0)
            return carry

        def tell_plane(index, carry):
            tell(0, index)
            return carry

        lax.fori_loop(1, RING, tell_ring, 0)
        lax.fori_loop(1, plane, tell_plane, 0)

    group_size = RING - 1 + plane - 1
    for peer in (up, down):
        pl.semaphore_signal(barrier, inc=1, device_id={"chan": peer}, device_id_type=MESH)
    pl.semaphore_signal(barrier, inc=1, device_id={"tm": 1 - core}, device_id_type=MESH)
    tell_group(barrier)
    for position in range(1, STEPS):
        for side in range(2):
            load(position, side).start()
    turn_copy.start()

    row = lax.broadcasted_iota(jnp.int32, (rows, fine), 0)
    sample = lax.broadcasted_iota(jnp.int32, (rows, fine), 1)
    spread = (row // 2 == sample).astype(F32)
    for p in range(TAPS):
        wide = jnp.broadcast_to(taps_ref[p : p + 1, :], (TILE, fine))
        taps_wide[p] = lax.dot_general(
            spread, wide, (((1,), (1,)), ((), ())),
            precision=lax.Precision.HIGHEST, preferred_element_type=F32,
        )

    keep = jnp.where(me == count - 1, 0.0, 1.0).astype(F32)
    group = 16
    width = 2 * FRAMES * TILE

    def filter_position(position):
        def filter_rows(step, carry):
            at = pl.ds(pl.multiple_of(step * group, group), group)
            taps = [taps_wide[p, at, :] for p in range(TAPS)]
            for side in range(2):
                series = [own_rows[side * STEPS + position, f, at, :].astype(F32) for f in range(FRAMES)]
                for f in range(FRAMES):
                    mine = taps[0] * series[f]
                    for p in range(1, f + 1):
                        mine = mine + taps[p] * series[f - p]
                    later = taps[f + 1] * series[FRAMES - 1]
                    for p in range(f + 2, TAPS):
                        later = later + taps[p] * series[FRAMES + f - p]
                    to = (side * FRAMES + f) * TILE
                    weighted[position, at, to : to + TILE] = mine.astype(BF16)
                    weighted[position, at, width + to : width + to + TILE] = (later * keep).astype(BF16)
            return carry

        lax.fori_loop(0, rows // group, filter_rows, 0)

    def transform(position, kind, entry, target, added=None):
        rows_at = slice(2 * plane * entry, 2 * plane * entry + near_rows)
        tiles = table_rows.shape[1]
        table = jnp.concatenate(
            [
                jnp.concatenate([table_rows[parity, tile, rows_at, :] for tile in range(tiles)], 1)
                for parity in range(2)
            ], 0,
        )
        for pair in range(FRAMES):
            base = kind * width + 2 * pair * TILE
            sums = jnp.dot(table, weighted[position, :, base : base + 2 * TILE], preferred_element_type=F32)
            for half in range(2):
                side, f = divmod(2 * pair + half, FRAMES)
                for parity in range(2):
                    one = sums[parity * near_rows : (parity + 1) * near_rows, half * TILE : (half + 1) * TILE]
                    if added is not None:
                        one = one + added[position, 1 - kind, side, parity, f].astype(F32)
                    target[position, kind, side, parity, f] = one.astype(BF16)

    def near(position):
        return [
            pltpu.make_async_remote_copy(
                part_send.at[position, kind], part_recv.at[position, kind],
                near_send.at[position, kind], near_recv.at[position, kind],
                device_id={"chan": peer}, device_id_type=MESH,
            )
            for kind, peer in enumerate((down, up))
        ]

    def prepare(position):
        for side in range(2):
            load(position, side).wait()
        filter_position(position)
        if position == 0:
            table_copy.wait()
        transform(position, 0, 0, part_send_rows)
        transform(position, 1, REACH + 1, part_send_rows)

    prepare(0)
    pl.semaphore_wait(barrier, group_size + 3)
    for position in range(STEPS):
        if position:
            prepare(position)
        for copy in near(position):
            copy.start()
        if position == 0:
            tell_group(met_sem)

    def extent(part):
        first, positions, side, sides, channel, channels = PARTS[part]
        return pl.ds(first, positions), pl.ds(side, sides), pl.ds(channel, channels)

    def send_part(part):
        at, sides, channels = extent(part)
        targets = [
            recv.at[at, sides, channels, pl.ds(FRAMES * block, FRAMES)] for block in (me, up)
        ]

        def source(kind, away, across):
            entry = away if kind == 0 else REACH - 1 - away
            return send.at[at, kind, sides, channels, :, entry * plane + lax.rem(column + across, plane)]

        for kind in range(2):
            pltpu.make_async_copy(source(kind, 0, 0), targets[kind], recv_sem.at[part]).start()

        def turn(index, carry):
            away, across = index // plane, lax.rem(index, plane)
            for kind, way in ((0, 1), (1, -1)):
                pltpu.make_async_remote_copy(
                    source(kind, away, across), targets[kind], send_sem.at[part], recv_sem.at[part],
                    device_id={"chan": chip(way * away, across)}, device_id_type=MESH,
                ).start()
            return carry

        lax.fori_loop(1, REACH * plane, turn, 0)

    for position in range(STEPS):
        for copy in near(position):
            copy.wait_recv()
        if position == 0:
            pl.semaphore_wait(met_sem, group_size)
        transform(position, 0, REACH, send_rows, part_recv_rows)
        transform(position, 1, 1, send_rows, part_recv_rows)
        for part in range(len(PARTS)):
            if PARTS[part][0] + PARTS[part][1] - 1 == position:
                send_part(part)
    turn_copy.wait()

    span = min(256, depth)

    def across(part):
        at, sides, channels = extent(part)
        return pltpu.make_async_remote_copy(
            recv.at[at, sides, channels], other.at[at, sides, channels], core_send.at[part], core_recv.at[part],
            device_id={"tm": 1 - core}, device_id_type=MESH,
        )

    def turn_part(part, source, base):
        first, positions, first_side, sides, channel, channels = PARTS[part]

        def turn_block(position, side):
            def one(parity, carry):
                for piece in range(depth // span):
                    flat = source[position, side, parity, piece * span : (piece + 1) * span, :].T
                    to = slice(base + piece * span, base + (piece + 1) * span)
                    left[side * STEPS + position, parity, 0:TILE, to] = flat
                    left[side * STEPS + position, parity, TILE : 2 * TILE, to] = jnp.dot(
                        flat, whole(turn_ref), preferred_element_type=F32
                    ).astype(BF16)
                return carry

            lax.fori_loop(channel, channel + channels, one, 0)

        for position in range(first, first + positions):
            for side in range(first_side, first_side + sides):
                block = BLOCKS[side][position]
                if block == 2:
                    turn_block(position, side)
                else:
                    pl.when(core == (0 if block < 2 else 1))(functools.partial(turn_block, position, side))

    def multiply_part(part, source, base):
        channel, channels = PARTS[part][4:]
        (total, other_total), codes = codes_of(part)

        def one_unit(step, carry):
            a, b, c = (lax.rem(code, 8) for code in carry[:3])
            slots = [lax.rem(code, 32) for code in carry[3:]]
            for parity in range(channel, channel + channels):
                right = jnp.concatenate(
                    [source[lax.rem(at, STEPS), at // STEPS, parity] for at in (b, c)], 1
                )
                sums = jnp.dot(left[a, parity, :, base : base + depth], right, preferred_element_type=F32)
                parts = []
                for index, slot in enumerate(slots):
                    weight = mask_ref[parity, slot + 18 * core].astype(F32) * scale
                    one = sums[:, index * TILE : (index + 1) * TILE].reshape(2, TILE, TILE) * weight
                    parts.append(one + out_ref[slot, parity] if base else one)
                for slot, one in zip(slots, parts):
                    out_ref[slot, parity] = one
            return tuple(code // 8 for code in carry[:3]) + tuple(code // 32 for code in carry[3:])

        start = tuple(low + core * (high - low) for low, high in zip(*codes))
        if total == other_total:
            lax.fori_loop(0, total, one_unit, start, unroll=total if total <= 3 else 1)
        else:
            lax.fori_loop(0, total + core * (other_total - total), one_unit, start)

    def finish(part):
        across(part).wait_recv()
        turn_part(part, other_rows, depth)
        multiply_part(part, other_rows, depth)

    for part in range(len(PARTS)):
        at, sides, channels = extent(part)
        arrived = recv.at[at, sides, channels]
        pltpu.make_async_copy(arrived, arrived, recv_sem.at[part]).wait()
        across(part).start()
        turn_part(part, recv_rows, 0)
        multiply_part(part, recv_rows, 0)
        finish(part)

    for part in range(len(PARTS)):
        at, sides, channels = extent(part)
        sent = send.at[at, :, sides, channels, :, pl.ds(0, REACH * plane - 1)]
        pltpu.make_async_copy(sent, sent, send_sem.at[part]).wait()
        across(part).wait_send()
    for position in range(STEPS):
        for copy in near(position):
            copy.wait_send()


def per_device(count, voltages, filter_taps, block_mask):
    fine = 2 * count
    frames = voltages.reshape(FRAMES, fine, 2, NBLK * TILE)
    depth = 2 * FRAMES * count
    span = min(256, depth)
    table, rotation = dft_table(fine), turn_table(span)
    dma = pltpu.SemaphoreType.DMA
    vmem = pl.BlockSpec(memory_space=pltpu.VMEM)
    anywhere = pl.BlockSpec(memory_space=pl.ANY)
    parts = len(PARTS)
    spectra = (STEPS, 2, 2, 2, FRAMES, REACH * (count // RING), 2, TILE)
    return pl.pallas_call(
        functools.partial(kernel, count),
        out_shape=pltpu.VMEM((18, 2, 2, TILE, TILE), F32),
        in_specs=[anywhere, vmem, anywhere, anywhere, pl.BlockSpec(memory_space=pltpu.SMEM)],
        out_specs=vmem,
        scratch_shapes=[
            pltpu.VMEM((NBLK, FRAMES, fine, 2, TILE), BF16),
            pltpu.VMEM((TAPS, 2 * fine, TILE), F32),
            pltpu.VMEM(table.shape[:2] + ((RING + 1) * (count // RING),) + table.shape[3:], BF16),
            pltpu.VMEM(rotation.shape, BF16),
            pltpu.VMEM((STEPS, 2 * fine, 4 * FRAMES * TILE), BF16),
            pltpu.VMEM(spectra, BF16),
            pltpu.VMEM(spectra, BF16),
            pltpu.VMEM(spectra, BF16),
            pltpu.VMEM((STEPS, 2, 2, FRAMES * count, 2, TILE), BF16),
            pltpu.VMEM((STEPS, 2, 2, FRAMES * count, 2, TILE), BF16),
            pltpu.VMEM((NBLK, 2, 2 * TILE, 2 * depth), BF16),
            dma((NBLK,)), dma((2,)), dma((STEPS, 2)), dma((STEPS, 2)), dma((parts,)), dma((parts,)),
            dma((parts,)), dma((parts,)), pltpu.SemaphoreType.REGULAR,
        ],
        compiler_params=pltpu.CompilerParams(
            collective_id=0, has_side_effects=True, vmem_limit_bytes=54 * 2**20
        ),
        cost_estimate=pl.CostEstimate(flops=6 * 10**9, bytes_accessed=10**7, transcendentals=0),
        name="correlate",
    )(frames, filter_taps, table, rotation, block_mask.T)


def solution(mesh):
    in_specs = (P("tm", "chan", None, None, None, None), P(), P(None, "chan"))
    out_specs = P("tm", "chan", None, None, None)
    return jax.shard_map(
        functools.partial(per_device, mesh.shape["chan"]),
        mesh=mesh, in_specs=in_specs, out_specs=out_specs, check_vma=False,
    )
```
